32 devices in a mesh: dp: 2 (over x), expert: 16 (over z, y, core).
Axes of the slice: x: 2, y: 2, z: 4, core: 2. Of those that a mesh axis runs over, the one named last changes fastest.
Arguments:
- tokens: bfloat16 [512, 4096], P('expert', 'dp'), may hold values from -6 to 6
- expert_ids: int32 [512, 8], P('expert'), may hold values from 0 to 15, all different within a row; in each aligned block of 32 rows (0 to 31, 32 to 63, ...) at most 32 rows name the same one
- route_weights: float32 [512, 8], P('expert'), may hold values from 0.1 to 1
- gate_weight: bfloat16 [16, 1536, 4096], P('expert', None, 'dp'), may hold values from -0.09375 to 0.09375
- up_weight: bfloat16 [16, 1536, 4096], P('expert', None, 'dp'), may hold values from -0.09375 to 0.09375
- down_weight: bfloat16 [16, 1536, 4096], P('expert', None, 'dp'), may hold values from -0.15625 to 0.15625
- output_grad: bfloat16 [512, 4096], P('expert', 'dp'), may hold values from -1.5 to 1.5
Outputs:
- layer_output: bfloat16 [512, 4096], P('expert', 'dp')
- token_gradient: bfloat16 [512, 4096], P('expert', 'dp')
- route_gradient: float32 [512, 8], P('expert')
- gate_gradient: bfloat16 [16, 1536, 4096], P('expert', None, 'dp')
- up_gradient: bfloat16 [16, 1536, 4096], P('expert', None, 'dp')
- down_gradient: bfloat16 [16, 1536, 4096], P('expert', None, 'dp')
The draws below stay inside these ranges and needn't reach their ends.
Inputs may be any that keep to these rules, and one draw needn't show every extreme that they name: `expert_ids`: within each aligned block of 32 tokens no expert is named more than 32 times, and in every draw some block names some expert exactly 32 times; the experts of one token differ.
All inputs are finite; a program needn't handle non-finite values.
Results may differ from the reference program's by a relative error of at most 0.023.
Values may be sent and summed in bfloat16 or wider, within the bound.
No kernel may reach another device: no remote copies, remote signals or barrier semaphores. Data moves between devices by JAX's collectives and lax.ppermute only.
A program may use at most 128 MiB of HBM per device.

```python
import math
import jax
import jax.numpy as jnp
import numpy as np
from jax import lax

D = 4096
HID = 1536
TOP = 8
TOK = 32
EXPERTS = 16
CAP = 32
TOKENS = 512
N_DP = 2
N_EXPERT = 16


def levels(stream_key, dims, pieces, smallest, top_value):
    def one(dim, parts):
        heights = jax.random.uniform(jax.random.fold_in(jax.random.fold_in(stream_key, 6), dim), (parts,), jnp.float32, smallest / len(pieces), top_value / len(pieces))
        return jnp.repeat(jnp.exp(heights), dims[dim] // parts).reshape((-1,) + (1,) * (len(dims) - dim - 1))

    factor_of = one(*pieces[0])
    for cut in pieces[1:]:
        factor_of = factor_of * one(*cut)
    return factor_of


def assign_block(stream_key, own, number, rows, number_of, top, bound, slope):
    ranking = jax.random.permutation(stream_key, number_of)
    heavy_load, ordinary = shares(number_of, rows * top, bound, slope, True), shares(number_of, rows * top, bound, slope, False)
    places = jnp.arange(number_of)

    def named(lengths, turn):
        used = int((lengths > 0).sum())
        fixed = max(1, used // 4)
        shifted = fixed + (places - fixed + turn * (used - fixed)) % max(1, number_of - fixed)
        return jnp.zeros((number_of,), jnp.int32).at[ranking[jnp.where(places < fixed, places, shifted)]].set(jnp.asarray(lengths, jnp.int32))

    lengths = jnp.where(number % 4 == 0, named(heavy_load, number // 4), named(ordinary, number - number // 4 - 1))
    mixed = jax.random.permutation(jax.random.fold_in(own, 3), number_of)
    source_of, taker = mixed[0:number_of // 2 * 2:2], mixed[1:number_of // 2 * 2:2]
    margin = jnp.minimum(lengths[source_of] - 1, bound - lengths[taker]) // 2
    margin = jnp.where((source_of == ranking[0]) | (taker == ranking[0]) | (lengths[taker] == 0), 0, jnp.maximum(margin, 0))
    shifted = jax.random.randint(jax.random.fold_in(own, 4), (number_of // 2,), 0, 1 << 20) % (margin + 1)
    lengths = lengths.at[source_of].add(-shifted).at[taker].add(shifted)
    labels = jnp.searchsorted(jnp.cumsum(lengths), jnp.arange(rows * top), side="right").astype(jnp.int32)
    grid = labels.reshape(top, rows).T
    grid = grid[jax.random.permutation(jax.random.fold_in(own, 1), rows)]
    turn = jax.random.randint(jax.random.fold_in(own, 2), (rows, 1), 0, top)
    return jnp.take_along_axis(grid, (jnp.arange(top)[None, :] + turn) % top, axis=1)


def shares(count, total, most, lean, full):
    portions = [(1 << 20) // math.isqrt(rank ** lean) + 1 for rank in range(1, count + 1)]
    largest = most if full else min(most, max(-(-total // count), total * portions[0] // sum(portions)))
    least = 1 if total - largest >= count - 1 else 0
    given, spare = [largest] + [least] * (count - 1), total - largest - least * (count - 1)
    while spare > 0:
        free = [i for i in range(1, count) if given[i] < largest] or [i for i in range(1, count) if given[i] < most]
        whole, remaining = sum([portions[i] for i in free]), spare
        for i in free:
            addition = min(most - given[i], max(1, remaining * portions[i] // whole), spare)
            given[i] = given[i] + addition
            spare = spare - addition
    return np.array(given)


def normal_values(own_key, extent, deviation, limit, shards=(), kind=jnp.bfloat16):
    array = deviation * jax.random.normal(own_key, extent, jnp.float32)
    if shards:
        array = array * levels(own_key, extent, shards, -0.22, 0.18)
    return jnp.clip(array, -limit, limit).astype(kind)


def setup_inputs(seed: int = 0) -> dict:
    seeds = jax.random.split(jax.random.key(seed), 8)
    tokens = normal_values(seeds[0], (TOKENS, D), 1.0, 6.0, ((0, 16), (1, 2)))
    expert_ids_keys = jax.random.split(jax.random.fold_in(seeds[1], 1), TOKENS // TOK)
    expert_ids_turns = jax.random.permutation(jax.random.fold_in(seeds[1], 3), TOKENS // TOK)
    expert_ids = jax.vmap(lambda own, number: assign_block(jax.random.fold_in(seeds[1], 2), own, number, TOK, EXPERTS, TOP, CAP, 2))(expert_ids_keys, expert_ids_turns).reshape((TOKENS, TOP))
    route_weights = jnp.clip(0.1 + 0.9 * jax.random.uniform(seeds[2], (TOKENS, TOP), jnp.float32) ** levels(seeds[2], (TOKENS, TOP), ((0, 16),), -0.2, 0.2), 0.1, 1.0)
    gate_weight = normal_values(seeds[3], (EXPERTS, HID, D), D ** -0.5, 0.09375, ((0, 16), (2, 2)))
    up_weight = normal_values(seeds[4], (EXPERTS, HID, D), D ** -0.5, 0.09375, ((0, 16), (2, 2)))
    down_weight = normal_values(seeds[5], (EXPERTS, HID, D), HID ** -0.5, 0.15625, ((0, 16), (2, 2)))
    output_grad = normal_values(seeds[6], (TOKENS, D), 0.25, 1.5, ((0, 16), (1, 2)))
    return {"tokens": tokens, "expert_ids": expert_ids, "route_weights": route_weights, "gate_weight": gate_weight, "up_weight": up_weight, "down_weight": down_weight, "output_grad": output_grad}


highest = lax.Precision.HIGHEST


def slot_tables(expert_ids):
    blocks = expert_ids.reshape(N_EXPERT, TOK * TOP)
    member = (blocks[:, :, None] == jnp.arange(EXPERTS, dtype=jnp.int32)[None, None, :]).astype(jnp.int32)
    before = jnp.cumsum(member, axis=1) - member
    rank_in = jnp.sum(before * member, axis=2)
    slot_ids = blocks * CAP + rank_in
    table = slot_ids[:, :, None] == jnp.arange(EXPERTS * CAP, dtype=jnp.int32)[None, None, :]
    return table.reshape(N_EXPERT, TOK, TOP, EXPERTS * CAP).astype(jnp.float32)


def block_sum(row_block, matrix):
    row_count = row_block.shape[0]
    width = D // N_DP
    rows = row_block.astype(jnp.float32).reshape(row_count, N_DP, width).transpose(1, 0, 2)
    cols = matrix.astype(jnp.float32).reshape(HID, N_DP, width).transpose(1, 0, 2)
    terms = jnp.einsum('srd,shd->srh', rows, cols, precision=highest)
    held = lax.optimization_barrier(terms.astype(jnp.bfloat16))
    return jnp.sum(held.astype(jnp.float32), axis=0)


def to_experts(spread, row_block):
    buffer = jnp.einsum('bts,btd->bsd', spread, row_block, precision=highest).astype(jnp.bfloat16)
    buffer = buffer.reshape(N_EXPERT, EXPERTS, CAP, D).transpose(1, 0, 2, 3)
    return buffer.reshape(EXPERTS, N_EXPERT * CAP, D)


def from_experts(row_block):
    row_block = row_block.reshape(EXPERTS, N_EXPERT, CAP, D).transpose(1, 0, 2, 3)
    return row_block.reshape(N_EXPERT, EXPERTS * CAP, D).astype(jnp.float32)


def expert_pass(operands):
    row_block, grad_block, gate_matrix, up_matrix, down_matrix = operands
    gate_pre = block_sum(row_block, gate_matrix)
    up_pre = block_sum(row_block, up_matrix)
    sigmoid_gate = jax.nn.sigmoid(gate_pre)
    silu_gate = gate_pre * sigmoid_gate
    hidden_act = (silu_gate * up_pre).astype(jnp.bfloat16)
    expert_out = jnp.dot(hidden_act, down_matrix, preferred_element_type=jnp.float32).astype(jnp.bfloat16)
    hidden_grad = block_sum(grad_block, down_matrix)
    silu_slope = sigmoid_gate * (1.0 + gate_pre * (1.0 - sigmoid_gate))
    gate_delta = (hidden_grad * up_pre * silu_slope).astype(jnp.bfloat16)
    up_delta = (hidden_grad * silu_gate).astype(jnp.bfloat16)
    down_gradient = jnp.dot(hidden_act.T, grad_block, preferred_element_type=jnp.float32).astype(jnp.bfloat16)
    gate_gradient = jnp.dot(gate_delta.T, row_block, preferred_element_type=jnp.float32).astype(jnp.bfloat16)
    up_gradient = jnp.dot(up_delta.T, row_block, preferred_element_type=jnp.float32).astype(jnp.bfloat16)
    back_out = jnp.dot(gate_delta, gate_matrix, preferred_element_type=jnp.float32)
    back_out = back_out + jnp.dot(up_delta, up_matrix, preferred_element_type=jnp.float32)
    back_out = back_out.astype(jnp.bfloat16)
    return expert_out, back_out, gate_gradient, up_gradient, down_gradient


def reference(tokens, expert_ids, route_weights, gate_weight, up_weight, down_weight, output_grad):
    table = slot_tables(expert_ids)
    picked = jnp.sum(table, axis=2)
    weights = route_weights.reshape(N_EXPERT, TOK, TOP)
    weighted = jnp.sum(table * weights[:, :, :, None], axis=2)
    dispatched = to_experts(picked, tokens.reshape(N_EXPERT, TOK, D).astype(jnp.float32))
    grads = output_grad.reshape(N_EXPERT, TOK, D).astype(jnp.float32)
    grad_dispatched = to_experts(weighted, grads)
    results = lax.map(expert_pass, (dispatched, grad_dispatched, gate_weight, up_weight, down_weight))
    expert_out, back_out, gate_gradient, up_gradient, down_gradient = results
    returned = from_experts(expert_out)
    layer_output = jnp.einsum('bts,bsd->btd', weighted, returned, precision=highest)
    layer_output = layer_output.astype(jnp.bfloat16).reshape(TOKENS, D)
    slot_grad = jnp.einsum('btd,bsd->bts', grads, returned, precision=highest)
    route_gradient = jnp.sum(table * slot_grad[:, :, None, :], axis=3).reshape(TOKENS, TOP)
    back_rows = from_experts(back_out)
    token_gradient = jnp.einsum('bts,bsd->btd', picked, back_rows, precision=highest)
    token_gradient = token_gradient.astype(jnp.bfloat16).reshape(TOKENS, D)
    return (layer_output, token_gradient, route_gradient, gate_gradient, up_gradient, down_gradient)
```

```python
import functools
import jax
import jax.numpy as jnp
from jax import lax
from jax.experimental import pallas as pl
from jax.experimental.pallas import tpu as pltpu
from jax.sharding import PartitionSpec as P

f32 = jnp.float32
bf16 = jnp.bfloat16
STEP = 256
ROOM = 12
IN_VMEM = pl.BlockSpec(memory_space=pltpu.VMEM)
IN_HBM = pl.BlockSpec(memory_space=pltpu.HBM)
IN_ANY = pl.BlockSpec(memory_space=pl.ANY)
IN_SMEM = pl.BlockSpec(memory_space=pltpu.SMEM)


def grant(mebibytes):
    return pltpu.CompilerParams(vmem_limit_bytes=mebibytes << 20)


def cost(flops=1 << 28):
    return pl.CostEstimate(flops=flops, bytes_accessed=1, transcendentals=0)


def tie(value, *earlier):
    return lax.optimization_barrier((value, *earlier))[0]


def shape(*dims, dtype=bf16):
    return jax.ShapeDtypeStruct(dims, dtype)


def flip(block, bit):
    count = lax.axis_size("expert")
    return lax.ppermute(block, "expert", [(i, i ^ bit) for i in range(count)])


def lowest_bit(number):
    return number & -number


def bits_of(number):
    return bin(number).count("1")


def split_bf16(value, pieces):
    out = []
    for _ in range(pieces):
        head = lax.reduce_precision(value, 8, 7)
        out.append(head.astype(bf16))
        value = value - head
    return out


def matmul(lhs, rhs):
    return lax.dot_general(lhs, rhs, (((1,), (0,)), ((), ())), preferred_element_type=f32)


def last_last(lhs, rhs):
    return lax.dot_general(lhs, rhs, (((1,), (1,)), ((), ())), preferred_element_type=f32)


def first_first(lhs, rhs):
    return lax.dot_general(lhs, rhs, (((0,), (0,)), ((), ())), preferred_element_type=f32)


def weight_columns(expert_ids, route_weights, experts):
    hit = expert_ids[:, :, None] == jnp.arange(experts, dtype=jnp.int32)[None, None, :]
    table = jnp.sum(jnp.where(hit, route_weights[:, :, None], 0.0), axis=1)
    columns = jnp.concatenate(split_bf16(table, 3) + [expert_ids.astype(bf16)], axis=1)
    return jnp.pad(columns, ((0, 0), (0, -columns.shape[1] % 128)))


class Blocks:
    def __init__(self, payload, experts, columns):
        self.arrays, self.place = [payload], {0: (0, 0)}
        self.experts, self.columns = experts, columns

    def add(self, array, offsets):
        self.arrays.append(array)
        for i, r in enumerate(offsets):
            self.place[r] = (len(self.arrays) - 1, i)

    def fetch(self, bit, offsets, after=()):
        array = self.joined([r ^ bit for r in offsets])
        self.add(flip(tie(array, *after), bit), offsets)

    def cores(self, evens, after=()):
        self.add(flip(tie(self.joined(evens), *after), 1), [r + 1 for r in evens])

    def joined(self, offsets):
        if offsets == [0]:
            return self.arrays[0]
        places = [self.place[r] for r in offsets]
        array = self.arrays[places[0][0]]
        assert places == [(places[0][0], i) for i in range(array.shape[0])]
        return array

    def join(self, offsets, after=()):
        arrays, places = self.use(offsets)
        made = pl.pallas_call(
            functools.partial(join_kernel, places),
            in_specs=[IN_ANY] * len(arrays),
            out_specs=IN_ANY,
            out_shape=shape(len(offsets), *arrays[0].shape[1:]),
            scratch_shapes=[pltpu.SemaphoreType.DMA((len(offsets),))],
            compiler_params=grant(ROOM),
            cost_estimate=cost(),
            name="join_blocks",
        )(tie(arrays[0], *after), *arrays[1:])
        self.add(made, offsets)
        return made

    def use(self, offsets):
        needed = sorted({self.place[r][0] for r in offsets})
        return [self.arrays[a] for a in needed], [
            (needed.index(self.place[r][0]), self.place[r][1]) for r in offsets
        ]


def join_kernel(places, *refs):
    data, out, sems = refs[:-2], refs[-2], refs[-1]
    copies = [pltpu.make_async_copy(data[a].at[j], out.at[i], sems.at[i]) for i, (a, j) in enumerate(places)]
    for copy in copies:
        copy.start()
    for copy in copies:
        copy.wait()


def load_kernel(places, count, *refs):
    data, sources, part = refs[:count], refs[count : count + 3], refs[count + 3]
    kept, (rows, sems, row_sems) = refs[count + 4 : count + 7], refs[-3:]
    size, width = data[0].shape[1], rows.shape[2]
    steps = sems.shape[1]
    many = sources[0].shape[0] // steps
    row_copies = [
        pltpu.make_async_copy(
            data[a].at[j, :, pl.ds(source * width, width)],
            rows.at[source, pl.ds(i * size, size)],
            row_sems.at[source, i],
        )
        for source in range(2)
        for i, (a, j) in enumerate(places)
    ]
    copies = {}
    for m in range(3):
        for t in range(steps):
            here = pl.ds(t * many, many)
            copies[m, t] = pltpu.make_async_copy(sources[m].at[here], kept[m].at[here], sems.at[m, t])
    for each in row_copies:
        each.start()
    for each in copies.values():
        each.start()
    for each in row_copies:
        each.wait()
    for m in range(3):
        for t in range(steps):
            copies[m, t].wait()
            here = slice(t * many, (t + 1) * many)
            part[m, :, here] = last_last(rows[int(m == 2)], kept[m][here, :]).astype(bf16)


def load_weights(blocks, offsets, weights):
    arrays, places = blocks.use(offsets)
    hidden, width = weights[0].shape
    count = len(offsets) * arrays[0].shape[1]
    out = pl.pallas_call(
        functools.partial(load_kernel, places, len(arrays)),
        in_specs=[IN_ANY] * (len(arrays) + 3),
        out_specs=[IN_VMEM] * 4,
        out_shape=[shape(3, count, hidden)] + [pltpu.VMEM((hidden, width), bf16)] * 3,
        scratch_shapes=[
            pltpu.VMEM((2, count, width), bf16),
            pltpu.SemaphoreType.DMA((3, 3)),
            pltpu.SemaphoreType.DMA((2, len(offsets))),
        ],
        compiler_params=grant(34),
        cost_estimate=cost(),
        name="load_weights",
    )(*arrays, *weights)
    return out[0], out[1:]


def part_kernel(places, pieces, count, *refs):
    data, weights = refs[:count], refs[count : count + 3]
    parts, (rows, sems) = refs[count + 3 : -2], refs[-2:]
    size, width = data[0].shape[1], rows.shape[2]
    used = sorted({int(m == 2) for _, which in pieces for m in which})
    copies = {}
    for source in used:
        for i, (a, j) in enumerate(places):
            copies[source, i] = pltpu.make_async_copy(
                data[a].at[j, :, pl.ds(source * width, width)],
                rows.at[source, pl.ds(i * size, size)],
                sems.at[source, i],
            )
    for copy in copies.values():
        copy.start()
    landed = set()
    for m in range(3):
        wanted = [(part, span, which.index(m)) for part, (span, which) in zip(parts, pieces) if m in which]
        if not wanted:
            continue
        source = int(m == 2)
        if source not in landed:
            landed.add(source)
            for i in range(len(places)):
                copies[source, i].wait()
        low = min(span[0] for _, span, _ in wanted)
        high = max(span[1] for _, span, _ in wanted)
        value = last_last(rows[source, low:high], weights[m][...]).astype(bf16)
        for part, (start, stop), slot in wanted:
            part[slot] = value[start - low : stop - low]


def partial_products(blocks, offsets, pieces, weights, after):
    arrays, places = blocks.use(offsets)
    size = arrays[0].shape[1]
    hidden, width = weights[0].shape
    count = len(offsets) * size
    pieces = [((start * size, stop * size), which) for start, stop, which in pieces]
    return pl.pallas_call(
        functools.partial(part_kernel, places, pieces, len(arrays)),
        in_specs=[IN_ANY] * len(arrays) + [IN_VMEM] * 3,
        out_specs=[IN_VMEM] * len(pieces),
        out_shape=[shape(len(which), stop - start, hidden) for (start, stop), which in pieces],
        scratch_shapes=[
            pltpu.VMEM((2, count, width), bf16),
            pltpu.SemaphoreType.DMA((2, len(offsets))),
        ],
        compiler_params=grant(ROOM),
        cost_estimate=cost(),
        name="partial_products",
    )(tie(arrays[0], *after), *arrays[1:], *weights)


def fetch_terms(layout, refs, front, back, meta, sems):
    segments, counts, count, places = layout
    pieces, at = [], 0
    for n in counts:
        pieces.append(refs[at : at + n])
        at += n
    data = refs[at : at + count]
    pairs = []
    for start, rows, p, p_row, q, slot, q_row in segments:
        for i, ref in enumerate(pieces[p]):
            pairs.append((ref.at[pl.ds(0, 2), pl.ds(p_row, rows)], front.at[i, :, pl.ds(start, rows)]))
        if back is not None:
            for i, ref in enumerate(pieces[q]):
                pairs.append((ref.at[slot, pl.ds(q_row, rows)], back.at[i, pl.ds(start, rows)]))
    size, columns = data[0].shape[1], data[0].shape[2]
    for i, (a, j) in enumerate(places):
        pairs.append(
            (
                data[a].at[j, :, pl.ds(columns - meta.shape[1], meta.shape[1])],
                meta.at[pl.ds(i * size, size)],
            )
        )
    copies = [pltpu.make_async_copy(*pair, sems.at[i]) for i, pair in enumerate(pairs)]
    for copy in copies:
        copy.start()
    return copies


def copies_of(layout, back):
    segments, counts, _, places = layout
    return (2 if back else 1) * counts[0] * len(segments) + len(places)


def own_weight(meta, experts, me):
    lane = lax.broadcasted_iota(jnp.int32, meta.shape, 1)
    mine = (lane == me) | (lane == me + experts) | (lane == me + 2 * experts)
    return jnp.sum(jnp.where(mine, meta[...].astype(f32), 0.0), axis=1, keepdims=True)


def act_kernel(layout, experts, me_ref, *refs):
    act, front, meta, sems = refs[-4:]
    for copy in fetch_terms(layout, refs[:-4], front, None, meta, sems):
        copy.wait()
    weight = own_weight(meta, experts, me_ref[0])
    for t in range(act.shape[1] // STEP):
        here = slice(t * STEP, (t + 1) * STEP)
        total = front[0, :, :, here].astype(f32)
        for i in range(1, front.shape[0]):
            total = total + front[i, :, :, here].astype(f32)
        gate_pre, up_pre = total[0], total[1]
        act[:, here] = (gate_pre * jax.nn.sigmoid(gate_pre) * up_pre * weight).astype(bf16)


def expert_kernel(layout, experts, parities, me_ref, *refs):
    segments, counts, count, places = layout
    inputs = sum(counts) + count
    gate, up, down, act, gate_delta, up_delta = refs[inputs : inputs + 6]
    results, (front, back, meta, sems) = refs[inputs + 6 : -4], refs[-4:]
    for copy in fetch_terms(layout, refs[:inputs], front, back, meta, sems):
        copy.wait()
    width = down.shape[1]
    size = meta.shape[0] // len(parities)
    me = me_ref[0]
    weight = own_weight(meta, experts, me)
    route = jnp.zeros(weight.shape, f32)
    for t in range(act.shape[1] // STEP):
        here = slice(t * STEP, (t + 1) * STEP)
        total, raw_grad = front[0, :, :, here].astype(f32), back[0, :, here].astype(f32)
        for i in range(1, front.shape[0]):
            total = total + front[i, :, :, here].astype(f32)
            raw_grad = raw_grad + back[i, :, here].astype(f32)
        gate_pre, up_pre = total[0], total[1]
        sigmoid_gate = jax.nn.sigmoid(gate_pre)
        silu_gate = gate_pre * sigmoid_gate
        product = silu_gate * up_pre
        hidden_grad = raw_grad * weight
        slope = sigmoid_gate * (1.0 + gate_pre * (1.0 - sigmoid_gate))
        act[:, here] = (product * weight).astype(bf16)
        gate_delta[:, here] = (hidden_grad * up_pre * slope).astype(bf16)
        up_delta[:, here] = (hidden_grad * silu_gate).astype(bf16)
        route = route + jnp.sum(product * raw_grad, axis=1, keepdims=True)

    def store(here, value):
        used = [0, 0]
        for i, odd in enumerate(parities):
            results[odd if len(results) > 1 else 0][used[odd] : used[odd] + size, here] = value[
                i * size : (i + 1) * size
            ]
            used[odd] += size

    tile = min(512, width)
    for t in range(width // tile):
        here = slice(t * tile, (t + 1) * tile)
        store(here, matmul(act[...], down[:, here]).astype(bf16))
        value = matmul(gate_delta[...], gate[:, here]) + matmul(up_delta[...], up[:, here])
        store(slice(width + t * tile, width + (t + 1) * tile), value.astype(bf16))
    columns = results[0].shape[1]
    lane = lax.broadcasted_iota(jnp.int32, (weight.shape[0], columns - 2 * width), 1)
    head = route.astype(bf16).astype(f32)
    spread = jnp.where(lane == me, head, jnp.where(lane == me + experts, route - head, 0.0))
    store(slice(2 * width, columns), spread.astype(bf16))


def expert_call(blocks, offsets, segments, pieces, plain, me, after, act_only=False):
    arrays, places = blocks.use(offsets)
    size = arrays[0].shape[1]
    hidden, width = plain[0].shape
    experts = blocks.experts
    meta_width = blocks.columns
    count = len(offsets) * size
    terms = [term for piece in pieces for term in piece]
    layout = (segments, [len(piece) for piece in pieces], len(arrays), places)
    kinds = len(pieces[0])
    scratch = [
        pltpu.VMEM((kinds, 2, count, hidden), bf16),
        pltpu.VMEM((kinds, count, hidden), bf16),
        pltpu.VMEM((count, meta_width), bf16),
        pltpu.SemaphoreType.DMA((copies_of(layout, not act_only),)),
    ]
    if act_only:
        return pl.pallas_call(
            functools.partial(act_kernel, layout, experts),
            in_specs=[IN_SMEM] + [IN_ANY] * (len(terms) + len(arrays)),
            out_specs=IN_VMEM,
            out_shape=shape(count, hidden),
            scratch_shapes=scratch[:1] + scratch[2:],
            compiler_params=grant(ROOM),
            cost_estimate=cost(),
            name="hidden_act",
        )(me, tie(terms[0], *after), *terms[1:], *arrays)
    parities = [r % 2 for r in offsets]
    columns = 2 * width + (2 * experts + 127) // 128 * 128
    halves = [shape(parities.count(p) * size, columns) for p in (0, 1) if parities.count(p)]
    return pl.pallas_call(
        functools.partial(expert_kernel, layout, experts, parities),
        in_specs=[IN_SMEM] + [IN_ANY] * (len(terms) + len(arrays)) + [IN_VMEM] * 3,
        out_specs=[IN_VMEM] * (3 + len(halves)),
        out_shape=[shape(count, hidden)] * 3 + halves,
        scratch_shapes=scratch,
        compiler_params=grant(ROOM if count <= 256 else 2 * ROOM),
        cost_estimate=cost(),
        name="expert_rows",
    )(me, tie(terms[0], *after), *terms[1:], *arrays, *plain)


def gradient_kernel(layout, *refs):
    places, column, sizes, kinds, count = layout
    chunks = refs[: kinds * len(sizes)]
    data = refs[kinds * len(sizes) :][:count]
    outs = refs[kinds * len(sizes) + count :][:kinds]
    rows, delta, tiles, sems, out_sems = refs[-5:]
    size, width = data[0].shape[1], rows.shape[1]
    copies = []
    for i, (a, j) in enumerate(places):
        copies.append((0, data[a].at[j, :, pl.ds(column, width)], rows.at[pl.ds(i * size, size)]))
    for kind in range(kinds):
        start = 0
        for i, many in enumerate(sizes):
            copies.append((kind, chunks[kind * len(sizes) + i], delta.at[kind, pl.ds(start, many)]))
            start += many
    copies = [(kind, pltpu.make_async_copy(*pair, sems.at[i])) for i, (kind, *pair) in enumerate(copies)]
    for _, copy in copies:
        copy.start()
    sent = []
    for kind in range(kinds):
        for owner, copy in copies:
            if owner == kind:
                copy.wait()
        for t in range(delta.shape[2] // STEP):
            k = len(sent)
            slot = k % tiles.shape[0]
            if k >= tiles.shape[0]:
                sent[k - tiles.shape[0]].wait()
            here = slice(t * STEP, (t + 1) * STEP)
            tiles[slot] = first_first(delta[kind, :, here], rows[...]).astype(bf16)
            copy = pltpu.make_async_copy(tiles.at[slot], outs[kind].at[pl.ds(t * STEP, STEP)], out_sems.at[k])
            copy.start()
            sent.append(copy)
    for copy in sent[-tiles.shape[0] :]:
        copy.wait()


def weight_gradients(blocks, offsets, deltas, column, width, room, after):
    arrays, places = blocks.use(offsets)
    hidden = deltas[0][0].shape[1]
    sizes = [d.shape[0] for d in deltas[0]]
    kinds, steps = len(deltas), hidden // STEP
    chunks = [d for kind in deltas for d in kind]
    return pl.pallas_call(
        functools.partial(gradient_kernel, (places, column, sizes, kinds, len(arrays))),
        in_specs=[IN_ANY] * (len(chunks) + len(arrays)),
        out_specs=[IN_ANY] * kinds,
        out_shape=[shape(hidden, width)] * kinds,
        scratch_shapes=[
            pltpu.VMEM((sum(sizes), width), bf16),
            pltpu.VMEM((kinds, sum(sizes), hidden), bf16),
            pltpu.VMEM((4, STEP, width), bf16),
            pltpu.SemaphoreType.DMA((len(places) + len(chunks),)),
            pltpu.SemaphoreType.DMA((kinds * steps,)),
        ],
        compiler_params=grant(room),
        cost_estimate=cost(1 << 32),
        name="weight_gradients",
    )(tie(chunks[0], *after), *chunks[1:], *arrays)


def swap(part):
    if lax.axis_size("dp") == 2:
        return [part, lax.ppermute(part, "dp", [(0, 1), (1, 0)])]
    return [lax.psum(part, "dp")]


def add_kernel(spans, left, right, *outs):
    for (left_row, right_row), out in zip(spans, outs):
        count = out.shape[0]
        total = left[left_row : left_row + count].astype(f32) + right[right_row : right_row + count].astype(f32)
        out[...] = total.astype(bf16)


def add_rows(left, right, spans, rows):
    return pl.pallas_call(
        functools.partial(add_kernel, spans),
        out_shape=[shape(rows, left.shape[1])] * len(spans),
        compiler_params=grant(ROOM),
        cost_estimate=cost(),
        name="add_rows",
    )(left, right)


def final_kernel(experts, payload, *refs):
    terms, (out, grad, route, meta, sem) = refs[:-5], refs[-5:]
    width, lanes = out.shape[1], meta.shape[1]
    copy = pltpu.make_async_copy(payload.at[0, :, pl.ds(payload.shape[2] - lanes, lanes)], meta, sem)
    copy.start()

    def total(here):
        value = terms[0][:, here].astype(f32)
        for term in terms[1:]:
            value = value + term[:, here].astype(f32)
        return value

    out[...] = total(slice(0, width)).astype(bf16)
    grad[...] = total(slice(width, 2 * width)).astype(bf16)
    table = total(slice(2 * width, terms[0].shape[1]))
    copy.wait()
    lane = lax.broadcasted_iota(jnp.int32, table.shape, 1)
    place = lax.broadcasted_iota(jnp.int32, route.shape, 1)
    found = jnp.zeros(route.shape, f32)
    for k in range(route.shape[1]):
        wanted = meta[:, 3 * experts + k : 3 * experts + k + 1].astype(jnp.int32)
        mine = (lane == wanted) | (lane == wanted + experts)
        value = jnp.sum(jnp.where(mine, table, 0.0), axis=1, keepdims=True)
        found = jnp.where(place == k, value, found)
    route[...] = found


def final_sums(payload, terms, width, chosen, experts, lanes):
    rows = payload.shape[1]
    return pl.pallas_call(
        functools.partial(final_kernel, experts),
        in_specs=[IN_ANY] + [IN_VMEM] * len(terms),
        out_shape=[shape(rows, width)] * 2 + [shape(rows, chosen, dtype=f32)],
        scratch_shapes=[pltpu.VMEM((rows, lanes), bf16), pltpu.SemaphoreType.DMA(())],
        compiler_params=grant(ROOM),
        cost_estimate=cost(),
        name="final_sums",
    )(payload, *terms)


def local(tokens, expert_ids, route_weights, gate_weight, up_weight, down_weight, output_grad):
    experts = lax.axis_size("expert")
    rows, width = tokens.shape
    me = lax.axis_index("expert").astype(jnp.int32).reshape(1)
    weights = [gate_weight[0], up_weight[0], down_weight[0]]
    columns = weight_columns(expert_ids, route_weights, experts)
    lanes = columns.shape[1]
    payload = tie(jnp.concatenate([tokens, output_grad, columns], axis=1)[None], me)

    def both(evens):
        return list(evens) + [e + 1 for e in evens]

    half = experts // 2
    first = [half]
    stages, held = [], [0, half]
    for bit in [1 << i for i in reversed(range(2, half.bit_length() - 1))]:
        stages.append([r ^ bit for r in held])
        held = held + stages[-1]
    early = [r for stage in stages for r in stage]
    late = [r ^ 2 for r in first + early]
    late = sorted(late, key=lambda r: (r ^ 2) in first)
    size = max(1, experts // 8)
    groups = [early] + [late[i : i + size] for i in range(0, len(late), size)] + [[2]]

    blocks = Blocks(payload, experts, lanes)
    blocks.cores([0])
    blocks.fetch(half, first)
    if len(stages) == 1:
        blocks.fetch(early[0], early[:1])
    part, plain = load_weights(blocks, [0, 1], weights)
    blocks.cores(first, after=[part])
    if len(stages) == 1:
        blocks.fetch(early[0], early[1:], after=[part])
    else:
        known = [0] + first
        for stage in stages:
            blocks.join(known)
            blocks.fetch(stage[0] ^ known[0], stage)
            known = known + stage

    clock = [0]
    after = [part]
    dues = []

    def step(kernel, *arguments, **options):
        clock[0] += 1
        now = [value for due, value in dues if due <= clock[0]]
        dues[:] = [each for each in dues if each[0] > clock[0]]
        made = kernel(*arguments, after=after + now, **options)
        after[:] = [made[0] if isinstance(made, (list, tuple)) else made]
        return made

    pieces, ranges = [], {}

    def send(made, offsets):
        pieces.append(swap(made))
        for i, r in enumerate(offsets):
            ranges[(r, len(made) == 1)] = (len(pieces) - 1, i * rows, len(made))

    def products(offsets, *wanted):
        wanted = wanted or ((0, len(offsets), (0, 1, 2)),)
        for made, (start, stop, _) in zip(step(partial_products, blocks, offsets, wanted, plain), wanted):
            send(made, offsets[start:stop])

    def rows_of(offsets, act_only=False):
        found, used = [], []
        for i, r in enumerate(offsets):
            front, front_row, _ = ranges[(r, False)]
            back, back_row, slots = ranges.get((r, True), ranges[(r, False)])
            if act_only:
                back, back_row, slots = front, front_row, 1
            for p in (front, back):
                if p not in used:
                    used.append(p)
            line = [i * rows, rows, used.index(front), front_row, used.index(back), slots - 1, back_row]
            last = found[-1] if found else None
            if (
                last
                and last[2] == line[2]
                and last[4] == line[4]
                and last[3] + last[1] == line[3]
                and last[6] + last[1] == line[6]
            ):
                last[1] += rows
            else:
                found.append(line)
        return tuple(tuple(line) for line in found), [pieces[p] for p in used]

    results, returned = [], []

    def expert_rows(evens, core_due=1, due=3):
        offsets = both(evens)
        act, gate_delta, up_delta, even, odd = step(
            expert_call, blocks, offsets, *rows_of(offsets), plain, me
        )
        results.append((act, gate_delta, up_delta))
        spans = [(i * rows, i * rows) for i in range(len(evens))]
        sums = add_rows(even, flip(odd, 1), spans, rows)
        dues.append((clock[0] + core_due, sums[0]))
        for r, value in zip(evens, sums):
            if r:
                value = flip(value, r)
                dues.append((clock[0] + due, value))
            returned.append(value)

    def wait_for(piece):
        after.extend(pieces[piece][1:])

    def arrived(piece):
        return pieces[piece][1:]

    send(part, [0, 1])
    products(both(first))
    source = [r ^ 2 for r in late]
    joined = blocks.join(early, after=after)
    blocks.cores(early, after=arrived(0))
    source_blocks = blocks.join(source, after=[joined])
    near = (len(early) + 1) // 2
    products(
        both(early[:near]) + both(early[near:]),
        (0, 2 * near, (0, 1, 2)),
        (2 * near, 2 * len(early), (0, 1, 2)),
    )
    blocks.fetch(2, late, after=after + arrived(1))
    blocks.cores(late, after=arrived(2))
    expert_rows([0] + first, due=2)
    rest, wanted = [], []
    for group in groups[1:-1]:
        wanted.append((len(rest), len(rest) + 2 * len(group), (0, 1, 2)))
        rest += both(group)
    products(rest, *wanted)
    blocks.fetch(2, [2], after=after)
    dues.append((clock[0] + 1, blocks.arrays[-1]))
    blocks.cores([2])
    expert_rows(early, due=2)
    products([2, 3], (0, 2, (0, 1)), (0, 2, (2,)))
    for i, group in enumerate(groups[1:-1]):
        expert_rows(group, due=6 if i == 0 else 5)
    order = both([0] + first) + [r for group in groups for r in both(group)]
    last = both([2])
    last_act = step(expert_call, blocks, last, *rows_of(last, True), plain, me, act_only=True)
    acts = [done[0] for done in results] + [last_act]
    (down_gradient,) = step(weight_gradients, blocks, order, [acts], width, width, 16)
    expert_rows([2], core_due=2, due=9)
    gate_deltas, up_deltas = ([done[kind] for done in results] for kind in (1, 2))
    (gate_gradient,) = step(weight_gradients, blocks, order, [gate_deltas], 0, width, 16)
    (up_gradient,) = step(weight_gradients, blocks, order, [up_deltas], 0, width, 58)
    layer_output, token_gradient, route_gradient = final_sums(
        payload, returned, width, expert_ids.shape[1], experts, lanes
    )
    return (
        layer_output,
        token_gradient,
        route_gradient,
        gate_gradient[None],
        up_gradient[None],
        down_gradient[None],
    )


def solution(mesh):
    by_token = P("expert", "dp")
    by_row = P("expert", None)
    by_weight = P("expert", None, "dp")
    return jax.shard_map(
        local,
        mesh=mesh,
        in_specs=(by_token, by_row, by_row, by_weight, by_weight, by_weight, by_token),
        out_specs=(by_token, by_token, by_row, by_weight, by_weight, by_weight),
        check_vma=False,
    )
```

```python
import functools
import jax
import jax.numpy as jnp
from jax import lax
from jax.experimental import pallas as pl
from jax.experimental.pallas import tpu as pltpu
from jax.sharding import PartitionSpec as P

f32 = jnp.float32
bf16 = jnp.bfloat16
STEP = 256
ROOM = 12
IN_VMEM = pl.BlockSpec(memory_space=pltpu.VMEM)
IN_HBM = pl.BlockSpec(memory_space=pltpu.HBM)
IN_ANY = pl.BlockSpec(memory_space=pl.ANY)
IN_SMEM = pl.BlockSpec(memory_space=pltpu.SMEM)


def grant(mebibytes):
    return pltpu.CompilerParams(vmem_limit_bytes=mebibytes << 20)


def cost(flops=1 << 28):
    return pl.CostEstimate(flops=flops, bytes_accessed=1, transcendentals=0)


def tie(value, *earlier):
    return lax.optimization_barrier((value, *earlier))[0]


def shape(*dims, dtype=bf16):
    return jax.ShapeDtypeStruct(dims, dtype)


def flip(block, bit):
    count = lax.axis_size("expert")
    return lax.ppermute(block, "expert", [(i, i ^ bit) for i in range(count)])


def lowest_bit(number):
    return number & -number


def bits_of(number):
    return bin(number).count("1")


def split_bf16(value, pieces):
    out = []
    for _ in range(pieces):
        head = lax.reduce_precision(value, 8, 7)
        out.append(head.astype(bf16))
        value = value - head
    return out


def matmul(lhs, rhs):
    return lax.dot_general(lhs, rhs, (((1,), (0,)), ((), ())), preferred_element_type=f32)


def last_last(lhs, rhs):
    return lax.dot_general(lhs, rhs, (((1,), (1,)), ((), ())), preferred_element_type=f32)


def first_first(lhs, rhs):
    return lax.dot_general(lhs, rhs, (((0,), (0,)), ((), ())), preferred_element_type=f32)


def weight_columns(expert_ids, route_weights, experts):
    hit = expert_ids[:, :, None] == jnp.arange(experts, dtype=jnp.int32)[None, None, :]
    table = jnp.sum(jnp.where(hit, route_weights[:, :, None], 0.0), axis=1)
    columns = jnp.concatenate(split_bf16(table, 3) + [expert_ids.astype(bf16)], axis=1)
    return jnp.pad(columns, ((0, 0), (0, -columns.shape[1] % 128)))


class Blocks:
    def __init__(self, payload, experts, columns):
        self.arrays, self.place = [payload], {0: (0, 0)}
        self.experts, self.columns = experts, columns

    def add(self, array, offsets):
        self.arrays.append(array)
        for i, r in enumerate(offsets):
            self.place[r] = (len(self.arrays) - 1, i)

    def fetch(self, bit, offsets, after=()):
        array = self.joined([r ^ bit for r in offsets])
        self.add(flip(tie(array, *after), bit), offsets)

    def cores(self, evens, after=()):
        self.add(flip(tie(self.joined(evens), *after), 1), [r + 1 for r in evens])

    def joined(self, offsets):
        if offsets == [0]:
            return self.arrays[0]
        places = [self.place[r] for r in offsets]
        array = self.arrays[places[0][0]]
        if places == [(places[0][0], i) for i in range(array.shape[0])]:
            return array
        return jnp.concatenate([self.arrays[a][i : i + 1] for a, i in places], axis=0)

    def join(self, offsets, after=()):
        arrays, places = self.use(offsets)
        made = pl.pallas_call(
            functools.partial(join_kernel, places),
            in_specs=[IN_ANY] * len(arrays),
            out_specs=IN_ANY,
            out_shape=shape(len(offsets), *arrays[0].shape[1:]),
            scratch_shapes=[pltpu.SemaphoreType.DMA((len(offsets),))],
            compiler_params=grant(ROOM),
            cost_estimate=cost(),
            name="join_blocks",
        )(tie(arrays[0], *after), *arrays[1:])
        self.add(made, offsets)
        return made

    def use(self, offsets):
        needed = sorted({self.place[r][0] for r in offsets})
        return [self.arrays[a] for a in needed], [
            (needed.index(self.place[r][0]), self.place[r][1]) for r in offsets
        ]


def join_kernel(places, *refs):
    data, out, sems = refs[:-2], refs[-2], refs[-1]
    copies = [pltpu.make_async_copy(data[a].at[j], out.at[i], sems.at[i]) for i, (a, j) in enumerate(places)]
    for copy in copies:
        copy.start()
    for copy in copies:
        copy.wait()


def load_kernel(places, count, *refs):
    data, sources, part = refs[:count], refs[count : count + 3], refs[count + 3]
    kept, (rows, sems, row_sems) = refs[count + 4 : count + 7], refs[-3:]
    size, width = data[0].shape[1], rows.shape[2]
    steps = sems.shape[1]
    many, total = sources[0].shape[0] // steps, rows.shape[1]
    row_copies = [
        pltpu.make_async_copy(
            data[a].at[j, :, pl.ds(source * width, width)],
            rows.at[source, pl.ds(i * size, size)],
            row_sems.at[source, i],
        )
        for source in range(2)
        for i, (a, j) in enumerate(places)
    ]
    copies = {}
    for m in range(3):
        for t in range(steps):
            here = pl.ds(t * many, many)
            copies[m, t] = pltpu.make_async_copy(sources[m].at[here], kept[m].at[here], sems.at[m, t])
    for each in row_copies:
        each.start()
    for each in copies.values():
        each.start()
    for each in row_copies:
        each.wait()
    for m in range(3):
        for t in range(steps):
            copies[m, t].wait()
            here = slice(t * many, (t + 1) * many)
            part[m * total : (m + 1) * total, here] = last_last(rows[int(m == 2)], kept[m][here, :]).astype(bf16)


def load_weights(blocks, offsets, weights):
    arrays, places = blocks.use(offsets)
    hidden, width = weights[0].shape
    count = len(offsets) * arrays[0].shape[1]
    out = pl.pallas_call(
        functools.partial(load_kernel, places, len(arrays)),
        in_specs=[IN_ANY] * (len(arrays) + 3),
        out_specs=[IN_VMEM] * 4,
        out_shape=[shape(3 * count, hidden)] + [pltpu.VMEM((hidden, width), bf16)] * 3,
        scratch_shapes=[
            pltpu.VMEM((2, count, width), bf16),
            pltpu.SemaphoreType.DMA((3, 3)),
            pltpu.SemaphoreType.DMA((2, len(offsets))),
        ],
        compiler_params=grant(34),
        cost_estimate=cost(),
        name="load_weights",
    )(*arrays, *weights)
    return out[0], out[1:]


def part_kernel(places, pieces, count, *refs):
    data, weights = refs[:count], refs[count : count + 3]
    parts, (rows, sems) = refs[count + 3 : -2], refs[-2:]
    size, width = data[0].shape[1], rows.shape[2]
    copies = {}
    for source in range(2):
        for i, (a, j) in enumerate(places):
            copies[source, i] = pltpu.make_async_copy(
                data[a].at[j, :, pl.ds(source * width, width)],
                rows.at[source, pl.ds(i * size, size)],
                sems.at[source, i],
            )
    for copy in copies.values():
        copy.start()
    for m in range(3):
        wanted = [
            (part, each) for part, piece in zip(parts, pieces) for each in piece if each[2] == m
        ]
        if m != 1:
            for i in range(len(places)):
                copies[int(m == 2), i].wait()
        if not wanted:
            continue
        low = min(each[0] for _, each in wanted)
        high = max(each[1] for _, each in wanted)
        value = last_last(rows[int(m == 2), low:high], weights[m][...]).astype(bf16)
        for part, (start, stop, _, base) in wanted:
            part[base : base + stop - start] = value[start - low : stop - low]


def partial_products(blocks, offsets, pieces, weights, after):
    arrays, places = blocks.use(offsets)
    size = arrays[0].shape[1]
    hidden, width = weights[0].shape
    count = len(offsets) * size
    spans, heights = [], []
    for piece in pieces:
        lines, base = [], 0
        for start, stop, m in piece:
            lines.append((start * size, stop * size, m, base))
            base += (stop - start) * size
        spans.append(lines)
        heights.append(base)
    return pl.pallas_call(
        functools.partial(part_kernel, places, spans, len(arrays)),
        in_specs=[IN_ANY] * len(arrays) + [IN_VMEM] * 3,
        out_specs=[IN_VMEM] * len(pieces),
        out_shape=[shape(height, hidden) for height in heights],
        scratch_shapes=[
            pltpu.VMEM((2, count, width), bf16),
            pltpu.SemaphoreType.DMA((2, len(offsets))),
        ],
        compiler_params=grant(ROOM if count <= 320 else 2 * ROOM),
        cost_estimate=cost(),
        name="partial_products",
    )(tie(arrays[0], *after), *arrays[1:], *weights)


def fetch_terms(layout, refs, terms, meta, sems):
    segments, counts, count, places = layout
    pieces, at = [], 0
    for n in counts:
        pieces.append(refs[at : at + n])
        at += n
    data = refs[at : at + count]
    pairs = []
    for m, start, rows, p, p_row in segments:
        for i, ref in enumerate(pieces[p]):
            pairs.append((ref.at[pl.ds(p_row, rows)], terms.at[i, m, pl.ds(start, rows)]))
    size, columns = data[0].shape[1], data[0].shape[2]
    for i, (a, j) in enumerate(places):
        pairs.append(
            (
                data[a].at[j, :, pl.ds(columns - meta.shape[1], meta.shape[1])],
                meta.at[pl.ds(i * size, size)],
            )
        )
    copies = [pltpu.make_async_copy(*pair, sems.at[i]) for i, pair in enumerate(pairs)]
    for copy in copies:
        copy.start()
    return copies


def own_weight(meta, experts, me):
    lane = lax.broadcasted_iota(jnp.int32, meta.shape, 1)
    mine = (lane == me) | (lane == me + experts) | (lane == me + 2 * experts)
    return jnp.sum(jnp.where(mine, meta[...].astype(f32), 0.0), axis=1, keepdims=True)


def expert_kernel(layout, experts, parities, me_ref, *refs):
    segments, counts, count, places = layout
    inputs = sum(counts) + count
    gate, up, down, act, gate_delta, up_delta = refs[inputs : inputs + 6]
    results, (terms, meta, sems) = refs[inputs + 6 : -3], refs[-3:]
    for copy in fetch_terms(layout, refs[:inputs], terms, meta, sems):
        copy.wait()
    width = down.shape[1]
    size = meta.shape[0] // len(parities)
    me = me_ref[0]
    weight = own_weight(meta, experts, me)
    route = jnp.zeros(weight.shape, f32)
    for t in range(act.shape[1] // STEP):
        here = slice(t * STEP, (t + 1) * STEP)
        total = terms[0, :, :, here].astype(f32)
        for i in range(1, terms.shape[0]):
            total = total + terms[i, :, :, here].astype(f32)
        gate_pre, up_pre, raw_grad = total[0], total[1], total[2]
        sigmoid_gate = jax.nn.sigmoid(gate_pre)
        silu_gate = gate_pre * sigmoid_gate
        product = silu_gate * up_pre
        hidden_grad = raw_grad * weight
        slope = sigmoid_gate * (1.0 + gate_pre * (1.0 - sigmoid_gate))
        act[:, here] = (product * weight).astype(bf16)
        gate_delta[:, here] = (hidden_grad * up_pre * slope).astype(bf16)
        up_delta[:, here] = (hidden_grad * silu_gate).astype(bf16)
        route = route + jnp.sum(product * raw_grad, axis=1, keepdims=True)

    def store(here, value):
        used = [0, 0]
        for i, odd in enumerate(parities):
            results[odd if len(results) > 1 else 0][used[odd] : used[odd] + size, here] = value[
                i * size : (i + 1) * size
            ]
            used[odd] += size

    tile = min(512, width)
    for t in range(width // tile):
        here = slice(t * tile, (t + 1) * tile)
        store(here, matmul(act[...], down[:, here]).astype(bf16))
        value = matmul(gate_delta[...], gate[:, here]) + matmul(up_delta[...], up[:, here])
        store(slice(width + t * tile, width + (t + 1) * tile), value.astype(bf16))
    columns = results[0].shape[1]
    lane = lax.broadcasted_iota(jnp.int32, (weight.shape[0], columns - 2 * width), 1)
    head = route.astype(bf16).astype(f32)
    spread = jnp.where(lane == me, head, jnp.where(lane == me + experts, route - head, 0.0))
    store(slice(2 * width, columns), spread.astype(bf16))


def expert_call(blocks, offsets, segments, pieces, plain, me, after):
    arrays, places = blocks.use(offsets)
    size = arrays[0].shape[1]
    hidden, width = plain[0].shape
    experts = blocks.experts
    meta_width = blocks.columns
    count = len(offsets) * size
    terms = [term for piece in pieces for term in piece]
    layout = (segments, [len(piece) for piece in pieces], len(arrays), places)
    kinds = len(pieces[0])
    scratch = [
        pltpu.VMEM((kinds, 3, count, hidden), bf16),
        pltpu.VMEM((count, meta_width), bf16),
        pltpu.SemaphoreType.DMA((kinds * len(segments) + len(places),)),
    ]
    parities = [r % 2 for r in offsets]
    columns = 2 * width + (2 * experts + 127) // 128 * 128
    halves = [shape(parities.count(p) * size, columns) for p in (0, 1) if parities.count(p)]
    return pl.pallas_call(
        functools.partial(expert_kernel, layout, experts, parities),
        in_specs=[IN_SMEM] + [IN_ANY] * (len(terms) + len(arrays)) + [IN_VMEM] * 3,
        out_specs=[IN_VMEM] * (3 + len(halves)),
        out_shape=[shape(count, hidden)] * 3 + halves,
        scratch_shapes=scratch,
        compiler_params=grant(ROOM if count <= 256 else 2 * ROOM),
        cost_estimate=cost(),
        name="expert_rows",
    )(me, tie(terms[0], *after), *terms[1:], *arrays, *plain)


def gradient_kernel(layout, *refs):
    places, column, sizes, count, before, ends = layout
    chunks, data = refs[: len(sizes)], refs[len(sizes) :][:count]
    earlier = refs[len(sizes) + count] if before else None
    out = refs[len(sizes) + count + before]
    rows, delta, tiles, sems, out_sems = refs[len(sizes) + count + before + 1 :]
    size, width = data[0].shape[1], rows.shape[1]
    pairs = []
    for i, (a, j) in enumerate(places):
        pairs.append((data[a].at[j, :, pl.ds(column, width)], rows.at[pl.ds(i * size, size)]))
    start = 0
    for ref, many in zip(chunks, sizes):
        pairs.append((ref, delta.at[pl.ds(start, many)]))
        start += many
    copies = [pltpu.make_async_copy(*pair, sems.at[i]) for i, pair in enumerate(pairs)]
    for copy in copies:
        copy.start()
    for copy in copies:
        copy.wait()
    sent = []
    for k in range(delta.shape[1] // STEP):
        here = slice(k * STEP, (k + 1) * STEP)
        value = first_first(delta[:, here], rows[...])
        if before:
            value = value + earlier[here, :].astype(f32)
        if not ends:
            out[here, :] = value.astype(bf16)
            continue
        slot = k % tiles.shape[0]
        if k >= tiles.shape[0]:
            sent[k - tiles.shape[0]].wait()
        tiles[slot] = value.astype(bf16)
        copy = pltpu.make_async_copy(tiles.at[slot], out.at[pl.ds(k * STEP, STEP)], out_sems.at[k])
        copy.start()
        sent.append(copy)
    for copy in sent[-tiles.shape[0] :]:
        copy.wait()


def weight_gradient(blocks, offsets, chunks, column, before, ends, after):
    arrays, places = blocks.use(offsets)
    hidden = chunks[0].shape[1]
    width = (arrays[0].shape[2] - blocks.columns) // 2
    sizes = [d.shape[0] for d in chunks]
    steps = hidden // STEP
    earlier = [] if before is None else [before]
    layout = (places, column * width, sizes, len(arrays), len(earlier), ends)
    return pl.pallas_call(
        functools.partial(gradient_kernel, layout),
        in_specs=[IN_ANY] * (len(chunks) + len(arrays)) + [IN_VMEM] * len(earlier),
        out_specs=IN_ANY if ends else IN_VMEM,
        out_shape=shape(hidden, width) if ends else pltpu.VMEM((hidden, width), bf16),
        scratch_shapes=[
            pltpu.VMEM((sum(sizes), width), bf16),
            pltpu.VMEM((sum(sizes), hidden), bf16),
            pltpu.VMEM((4 if ends else 1, STEP, width), bf16),
            pltpu.SemaphoreType.DMA((len(places) + len(chunks),)),
            pltpu.SemaphoreType.DMA((steps,)),
        ],
        compiler_params=grant(ROOM if ends else 8),
        cost_estimate=cost(1 << 31 if ends else 1 << 28),
        name="weight_gradient",
    )(tie(chunks[0], *after), *chunks[1:], *arrays, *earlier)


def swap(part):
    if lax.axis_size("dp") == 2:
        return [part, lax.ppermute(part, "dp", [(0, 1), (1, 0)])]
    return [lax.psum(part, "dp")]


def add_kernel(spans, left, right, *outs):
    for (left_row, right_row), out in zip(spans, outs):
        count = out.shape[0]
        total = left[left_row : left_row + count].astype(f32) + right[right_row : right_row + count].astype(f32)
        out[...] = total.astype(bf16)


def add_rows(left, right, spans, rows):
    return pl.pallas_call(
        functools.partial(add_kernel, spans),
        out_shape=[shape(rows, left.shape[1])] * len(spans),
        compiler_params=grant(ROOM),
        cost_estimate=cost(),
        name="add_rows",
    )(left, right)


def final_kernel(experts, payload, *refs):
    terms, (out, grad, route, meta, sem) = refs[:-5], refs[-5:]
    width, lanes = out.shape[1], meta.shape[1]
    copy = pltpu.make_async_copy(payload.at[0, :, pl.ds(payload.shape[2] - lanes, lanes)], meta, sem)
    copy.start()

    def total(here):
        value = terms[0][:, here].astype(f32)
        for term in terms[1:]:
            value = value + term[:, here].astype(f32)
        return value

    out[...] = total(slice(0, width)).astype(bf16)
    grad[...] = total(slice(width, 2 * width)).astype(bf16)
    table = total(slice(2 * width, terms[0].shape[1]))
    copy.wait()
    lane = lax.broadcasted_iota(jnp.int32, table.shape, 1)
    found = jnp.zeros(table.shape, f32)
    for k in range(route.shape[0]):
        wanted = meta[:, 3 * experts + k : 3 * experts + k + 1].astype(jnp.int32)
        mine = (lane == wanted) | (lane == wanted + experts)
        value = jnp.sum(jnp.where(mine, table, 0.0), axis=1, keepdims=True)
        found = jnp.where(lane == k, value, found)
    route[...] = found.T[: route.shape[0]]


def final_sums(payload, terms, width, chosen, experts, lanes):
    rows = payload.shape[1]
    return pl.pallas_call(
        functools.partial(final_kernel, experts),
        in_specs=[IN_ANY] + [IN_VMEM] * len(terms),
        out_shape=[shape(rows, width)] * 2 + [shape(chosen, rows, dtype=f32)],
        scratch_shapes=[pltpu.VMEM((rows, lanes), bf16), pltpu.SemaphoreType.DMA(())],
        compiler_params=grant(ROOM),
        cost_estimate=cost(),
        name="final_sums",
    )(payload, *terms)


def local(tokens, expert_ids, route_weights, gate_weight, up_weight, down_weight, output_grad):
    experts = lax.axis_size("expert")
    rows, width = tokens.shape
    me = lax.axis_index("expert").astype(jnp.int32).reshape(1)
    weights = [gate_weight[0], up_weight[0], down_weight[0]]
    columns = weight_columns(expert_ids, route_weights, experts)
    lanes = columns.shape[1]
    payload = tie(jnp.concatenate([tokens, output_grad, columns], axis=1)[None], me)

    def both(evens):
        return list(evens) + [e + 1 for e in evens]

    half = experts // 2
    first = [half]
    stages, held = [], [0, half]
    for bit in [1 << i for i in reversed(range(2, half.bit_length() - 1))]:
        stages.append([r ^ bit for r in held])
        held = held + stages[-1]
    early = [r for stage in stages for r in stage]
    if len(stages) == 1:
        near, far = sorted(early)
        lead, groups = [far], [[far, far ^ 2], [near, half ^ 2], [near ^ 2, 2]]
    else:
        lead, size = stages[0], experts // 8
        rest = [r for r in early if r not in lead] + [r ^ 2 for r in first + early] + [2]
        groups = [lead] + [rest[i : i + size] for i in range(0, len(rest), size)]
    rest = [r for group in groups for r in group if r not in lead]

    blocks = Blocks(payload, experts, lanes)
    blocks.cores([0])
    blocks.fetch(half, first)
    blocks.fetch(2, [2])
    if len(stages) == 1:
        blocks.fetch(near, [near])
    part, plain = load_weights(blocks, [0, 1], weights)
    blocks.cores(first, after=[part] + blocks.arrays[2:])
    if len(stages) == 1:
        blocks.fetch(near, [far], after=[part])
    else:
        known = [0] + first
        for stage in stages:
            blocks.join(known)
            blocks.fetch(stage[0] ^ known[0], stage)
            known = known + stage
    blocks.fetch(2, [half ^ 2], after=[part])
    gate = blocks.arrays[-1:]
    if len(stages) == 1:
        blocks.fetch(2, [near ^ 2], after=[part])
        gate = blocks.arrays[-2:]

    clock = [0]
    after = [part]
    dues = []

    def step(kernel, *arguments, **options):
        clock[0] += 1
        now = [value for due, value in dues if due <= clock[0]]
        dues[:] = [each for each in dues if each[0] > clock[0]]
        made = kernel(*arguments, after=after + now, **options)
        after[:] = [made[0] if isinstance(made, (list, tuple)) else made]
        return made

    pieces, lines = [], {}

    def send(made, offsets, piece):
        pieces.append(swap(made))
        base = 0
        for start, stop, m in piece:
            for r in offsets[start:stop]:
                lines[(r, m)] = (len(pieces) - 1, base)
                base += rows

    def whole(start, stop):
        return [(start, stop, m) for m in range(3)]

    def products(offsets, *wanted):
        wanted = wanted or (whole(0, len(offsets)),)
        for made, piece in zip(step(partial_products, blocks, offsets, wanted, plain), wanted):
            send(made, offsets, piece)

    def terms_of(offsets):
        found, used = [], []
        for m in range(3):
            for i, r in enumerate(offsets):
                piece, row = lines[(r, m)]
                if piece not in used:
                    used.append(piece)
                last = found[-1] if found else None
                if last and (last[0], last[3], last[4] + last[2]) == (m, used.index(piece), row):
                    last[2] += rows
                else:
                    found.append([m, i * rows, rows, used.index(piece), row])
        return tuple(tuple(line) for line in found), [pieces[p] for p in used]

    results, returned, summed = [], [], []

    def expert_rows(evens, core_due=None, due=None, gate=(), send_gate=()):
        offsets = both(evens)
        act, gate_delta, up_delta, even, odd = step(
            expert_call, blocks, offsets, *terms_of(offsets), plain, me
        )
        results.append((act, gate_delta, up_delta))
        spans = [(i * rows, i * rows) for i in range(len(evens))]
        sums = add_rows(even, flip(tie(odd, *gate), 1), spans, rows)
        if core_due:
            dues.append((clock[0] + core_due, sums[0]))
        for r, value in zip(evens, sums):
            if r:
                value = flip(tie(value, *send_gate), r)
                if due:
                    dues.append((clock[0] + due, value))
            returned.append(value)

    def arrived(piece):
        return pieces[piece][1:]

    def arrived(piece):
        return pieces[piece][1:]

    def halves(start, stop):
        middle = (start + stop + 1) // 2
        return [whole(start, middle), whole(middle, stop)]

    send(part, [0, 1], whole(0, 2))
    products(both(first))
    for run in [[far]] if len(stages) == 1 else stages:
        blocks.fetch(2, [r ^ 2 for r in run], after=arrived(0))
    blocks.cores(lead, after=gate)

    def paired(evens):
        return [r for e in evens for r in (e, e + 1)]

    products(paired(lead))
    blocks.join(rest, after=after)
    blocks.cores(rest, after=arrived(1))
    wanted, leads, at = [], [], 0
    for group in groups:
        last = group is groups[-1]
        group = [r for r in group if r not in lead]
        leads.append(3 + len(wanted))
        if len(group) > 1:
            wanted += halves(at, at + 2 * len(group))
        elif group:
            wanted.append(whole(at, at + 2 * len(group)))
        at += 2 * len(group)
    expert_rows([0] + first, due=2, send_gate=arrived(2))
    products(paired(rest), *wanted)
    worked = both([0] + first)
    gradients = [None] * 3

    def add_gradients(offsets, chunks_from, kinds, ends):
        for kind in kinds:
            chunks = [done[kind] for done in results[chunks_from:]]
            gradients[kind] = step(
                weight_gradient, blocks, offsets, chunks, int(kind == 0), gradients[kind], ends
            )

    for i, group in enumerate(groups):
        left = len(groups) - 1 - i
        if left == 1:
            add_gradients(worked, 0, (1, 2), False)
            summed_rows, summed_chunks = len(worked), len(results)
        if left == 0:
            expert_rows(group, core_due=2)
        else:
            gate = arrived(leads[i + 1]) + (sent if left == 1 else [])
            expert_rows(group, core_due=1 if left == 1 else None, due=4 if left == 1 else None, gate=gate)
            sent = returned[-len(group) :]
        worked = worked + both(group)
    add_gradients(worked[summed_rows:], summed_chunks, (1, 2), True)
    add_gradients(worked, 0, (0,), True)
    down_gradient, gate_gradient, up_gradient = gradients
    layer_output, token_gradient, route_gradient = final_sums(
        payload, returned, width, expert_ids.shape[1], experts, lanes
    )
    return (
        layer_output,
        token_gradient,
        route_gradient.T,
        gate_gradient[None],
        up_gradient[None],
        down_gradient[None],
    )


def solution(mesh):
    by_token = P("expert", "dp")
    by_row = P("expert", None)
    by_weight = P("expert", None, "dp")
    return jax.shard_map(
        local,
        mesh=mesh,
        in_specs=(by_token, by_row, by_row, by_weight, by_weight, by_weight, by_token),
        out_specs=(by_token, by_token, by_row, by_weight, by_weight, by_weight),
        check_vma=False,
    )
```

```python
import functools
import jax
import jax.numpy as jnp
from jax import lax
from jax.experimental import pallas as pl
from jax.experimental.pallas import tpu as pltpu
from jax.sharding import PartitionSpec as P

f32 = jnp.float32
bf16 = jnp.bfloat16
STEP = 256
ROOM = 12
IN_VMEM = pl.BlockSpec(memory_space=pltpu.VMEM)
IN_HBM = pl.BlockSpec(memory_space=pltpu.HBM)
IN_ANY = pl.BlockSpec(memory_space=pl.ANY)
IN_SMEM = pl.BlockSpec(memory_space=pltpu.SMEM)


def grant(mebibytes):
    return pltpu.CompilerParams(vmem_limit_bytes=mebibytes << 20)


def cost(flops=1 << 28):
    return pl.CostEstimate(flops=flops, bytes_accessed=1, transcendentals=0)


def tie(value, *earlier):
    return lax.optimization_barrier((value, *earlier))[0]


def shape(*dims, dtype=bf16):
    return jax.ShapeDtypeStruct(dims, dtype)


def flip(block, bit):
    count = lax.axis_size("expert")
    return lax.ppermute(block, "expert", [(i, i ^ bit) for i in range(count)])


def lowest_bit(number):
    return number & -number


def bits_of(number):
    return bin(number).count("1")


def split_bf16(value, pieces):
    out = []
    for _ in range(pieces):
        head = lax.reduce_precision(value, 8, 7)
        out.append(head.astype(bf16))
        value = value - head
    return out


def matmul(lhs, rhs):
    return lax.dot_general(lhs, rhs, (((1,), (0,)), ((), ())), preferred_element_type=f32)


def last_last(lhs, rhs):
    return lax.dot_general(lhs, rhs, (((1,), (1,)), ((), ())), preferred_element_type=f32)


def first_first(lhs, rhs):
    return lax.dot_general(lhs, rhs, (((0,), (0,)), ((), ())), preferred_element_type=f32)


def weight_columns(expert_ids, route_weights, experts):
    hit = expert_ids[:, :, None] == jnp.arange(experts, dtype=jnp.int32)[None, None, :]
    table = jnp.sum(jnp.where(hit, route_weights[:, :, None], 0.0), axis=1)
    columns = jnp.concatenate(split_bf16(table, 3) + [expert_ids.astype(bf16)], axis=1)
    return jnp.pad(columns, ((0, 0), (0, -columns.shape[1] % 128)))


class Blocks:
    def __init__(self, payload, experts, columns):
        self.arrays, self.place = [payload], {0: (0, 0)}
        self.experts, self.columns = experts, columns

    def add(self, array, offsets):
        self.arrays.append(array)
        for i, r in enumerate(offsets):
            self.place[r] = (len(self.arrays) - 1, i)

    def fetch(self, bit, offsets, after=()):
        array = self.joined([r ^ bit for r in offsets])
        self.add(flip(tie(array, *after), bit), offsets)

    def cores(self, evens, after=()):
        self.add(flip(tie(self.joined(evens), *after), 1), [r + 1 for r in evens])

    def joined(self, offsets):
        if offsets == [0]:
            return self.arrays[0]
        places = [self.place[r] for r in offsets]
        array = self.arrays[places[0][0]]
        if places == [(places[0][0], i) for i in range(array.shape[0])]:
            return array
        return jnp.concatenate([self.arrays[a][i : i + 1] for a, i in places], axis=0)

    def join(self, offsets, after=()):
        arrays, places = self.use(offsets)
        made = pl.pallas_call(
            functools.partial(join_kernel, places),
            in_specs=[IN_ANY] * len(arrays),
            out_specs=IN_ANY,
            out_shape=shape(len(offsets), *arrays[0].shape[1:]),
            scratch_shapes=[pltpu.SemaphoreType.DMA((len(offsets),))],
            compiler_params=grant(ROOM),
            cost_estimate=cost(),
            name="join_blocks",
        )(tie(arrays[0], *after), *arrays[1:])
        self.add(made, offsets)
        return made

    def use(self, offsets):
        needed = sorted({self.place[r][0] for r in offsets})
        return [self.arrays[a] for a in needed], [
            (needed.index(self.place[r][0]), self.place[r][1]) for r in offsets
        ]


def join_kernel(places, *refs):
    data, out, sems = refs[:-2], refs[-2], refs[-1]
    copies = [pltpu.make_async_copy(data[a].at[j], out.at[i], sems.at[i]) for i, (a, j) in enumerate(places)]
    for copy in copies:
        copy.start()
    for copy in copies:
        copy.wait()


def load_kernel(places, count, *refs):
    data, sources, part = refs[:count], refs[count : count + 3], refs[count + 3]
    kept, (rows, sems, row_sems) = refs[count + 4 : count + 7], refs[-3:]
    size, width = data[0].shape[1], rows.shape[2]
    steps = sems.shape[1]
    many, total = sources[0].shape[0] // steps, rows.shape[1]
    row_copies = [
        pltpu.make_async_copy(
            data[a].at[j, :, pl.ds(source * width, width)],
            rows.at[source, pl.ds(i * size, size)],
            row_sems.at[source, i],
        )
        for source in range(2)
        for i, (a, j) in enumerate(places)
    ]
    copies = {}
    for m in range(3):
        for t in range(steps):
            here = pl.ds(t * many, many)
            copies[m, t] = pltpu.make_async_copy(sources[m].at[here], kept[m].at[here], sems.at[m, t])
    for each in row_copies:
        each.start()
    for each in copies.values():
        each.start()
    for each in row_copies:
        each.wait()
    for m in range(3):
        for t in range(steps):
            copies[m, t].wait()
            here = slice(t * many, (t + 1) * many)
            part[m * total : (m + 1) * total, here] = last_last(rows[int(m == 2)], kept[m][here, :]).astype(bf16)


def load_weights(blocks, offsets, weights):
    arrays, places = blocks.use(offsets)
    hidden, width = weights[0].shape
    count = len(offsets) * arrays[0].shape[1]
    out = pl.pallas_call(
        functools.partial(load_kernel, places, len(arrays)),
        in_specs=[IN_ANY] * (len(arrays) + 3),
        out_specs=[IN_VMEM] * 4,
        out_shape=[shape(3 * count, hidden)] + [pltpu.VMEM((hidden, width), bf16)] * 3,
        scratch_shapes=[
            pltpu.VMEM((2, count, width), bf16),
            pltpu.SemaphoreType.DMA((3, 3)),
            pltpu.SemaphoreType.DMA((2, len(offsets))),
        ],
        compiler_params=grant(34),
        cost_estimate=cost(),
        name="load_weights",
    )(*arrays, *weights)
    return out[0], out[1:]


def part_kernel(places, pieces, count, *refs):
    data, weights = refs[:count], refs[count : count + 3]
    parts, (rows, sems) = refs[count + 3 : -2], refs[-2:]
    size, width = data[0].shape[1], rows.shape[2]
    copies = {}
    for source in range(2):
        for i, (a, j) in enumerate(places):
            copies[source, i] = pltpu.make_async_copy(
                data[a].at[j, :, pl.ds(source * width, width)],
                rows.at[source, pl.ds(i * size, size)],
                sems.at[source, i],
            )
    for copy in copies.values():
        copy.start()
    for m in range(3):
        wanted = [
            (part, each) for part, piece in zip(parts, pieces) for each in piece if each[2] == m
        ]
        if m != 1:
            for i in range(len(places)):
                copies[int(m == 2), i].wait()
        if not wanted:
            continue
        low = min(each[0] for _, each in wanted)
        high = max(each[1] for _, each in wanted)
        value = last_last(rows[int(m == 2), low:high], weights[m][...]).astype(bf16)
        for part, (start, stop, _, base) in wanted:
            part[base : base + stop - start] = value[start - low : stop - low]


def partial_products(blocks, offsets, pieces, weights, after):
    arrays, places = blocks.use(offsets)
    size = arrays[0].shape[1]
    hidden, width = weights[0].shape
    count = len(offsets) * size
    spans, heights = [], []
    for piece in pieces:
        lines, base = [], 0
        for start, stop, m in piece:
            lines.append((start * size, stop * size, m, base))
            base += (stop - start) * size
        spans.append(lines)
        heights.append(base)
    return pl.pallas_call(
        functools.partial(part_kernel, places, spans, len(arrays)),
        in_specs=[IN_ANY] * len(arrays) + [IN_VMEM] * 3,
        out_specs=[IN_VMEM] * len(pieces),
        out_shape=[shape(height, hidden) for height in heights],
        scratch_shapes=[
            pltpu.VMEM((2, count, width), bf16),
            pltpu.SemaphoreType.DMA((2, len(offsets))),
        ],
        compiler_params=grant(ROOM if count <= 320 else 2 * ROOM),
        cost_estimate=cost(),
        name="partial_products",
    )(tie(arrays[0], *after), *arrays[1:], *weights)


def fetch_terms(layout, refs, terms, meta, sems):
    segments, counts, count, places = layout
    pieces, at = [], 0
    for n in counts:
        pieces.append(refs[at : at + n])
        at += n
    data = refs[at : at + count]
    pairs = []
    for m, start, rows, p, p_row in segments:
        for i, ref in enumerate(pieces[p]):
            pairs.append((ref.at[pl.ds(p_row, rows)], terms.at[i, m, pl.ds(start, rows)]))
    size, columns = data[0].shape[1], data[0].shape[2]
    for i, (a, j) in enumerate(places):
        pairs.append(
            (
                data[a].at[j, :, pl.ds(columns - meta.shape[1], meta.shape[1])],
                meta.at[pl.ds(i * size, size)],
            )
        )
    copies = [pltpu.make_async_copy(*pair, sems.at[i]) for i, pair in enumerate(pairs)]
    for copy in copies:
        copy.start()
    return copies


def own_weight(meta, experts, me):
    lane = lax.broadcasted_iota(jnp.int32, meta.shape, 1)
    mine = (lane == me) | (lane == me + experts) | (lane == me + 2 * experts)
    return jnp.sum(jnp.where(mine, meta[...].astype(f32), 0.0), axis=1, keepdims=True)


def expert_kernel(layout, experts, parities, me_ref, *refs):
    segments, counts, count, places = layout
    inputs = sum(counts) + count
    gate, up, down, act, gate_delta, up_delta = refs[inputs : inputs + 6]
    results, (terms, meta, sems) = refs[inputs + 6 : -3], refs[-3:]
    for copy in fetch_terms(layout, refs[:inputs], terms, meta, sems):
        copy.wait()
    width = down.shape[1]
    size = meta.shape[0] // len(parities)
    me = me_ref[0]
    weight = own_weight(meta, experts, me)
    route = jnp.zeros(weight.shape, f32)
    for t in range(act.shape[1] // STEP):
        here = slice(t * STEP, (t + 1) * STEP)
        total = terms[0, :, :, here].astype(f32)
        for i in range(1, terms.shape[0]):
            total = total + terms[i, :, :, here].astype(f32)
        gate_pre, up_pre, raw_grad = total[0], total[1], total[2]
        sigmoid_gate = jax.nn.sigmoid(gate_pre)
        silu_gate = gate_pre * sigmoid_gate
        product = silu_gate * up_pre
        hidden_grad = raw_grad * weight
        slope = sigmoid_gate * (1.0 + gate_pre * (1.0 - sigmoid_gate))
        act[:, here] = (product * weight).astype(bf16)
        gate_delta[:, here] = (hidden_grad * up_pre * slope).astype(bf16)
        up_delta[:, here] = (hidden_grad * silu_gate).astype(bf16)
        route = route + jnp.sum(product * raw_grad, axis=1, keepdims=True)

    def store(here, value):
        used = [0, 0]
        for i, odd in enumerate(parities):
            results[odd if len(results) > 1 else 0][used[odd] : used[odd] + size, here] = value[
                i * size : (i + 1) * size
            ]
            used[odd] += size

    tile = min(512, width)
    for t in range(width // tile):
        here = slice(t * tile, (t + 1) * tile)
        store(here, matmul(act[...], down[:, here]).astype(bf16))
        value = matmul(gate_delta[...], gate[:, here]) + matmul(up_delta[...], up[:, here])
        store(slice(width + t * tile, width + (t + 1) * tile), value.astype(bf16))
    columns = results[0].shape[1]
    lane = lax.broadcasted_iota(jnp.int32, (weight.shape[0], columns - 2 * width), 1)
    head = route.astype(bf16).astype(f32)
    spread = jnp.where(lane == me, head, jnp.where(lane == me + experts, route - head, 0.0))
    store(slice(2 * width, columns), spread.astype(bf16))


def expert_call(blocks, offsets, segments, pieces, plain, me, after):
    arrays, places = blocks.use(offsets)
    size = arrays[0].shape[1]
    hidden, width = plain[0].shape
    experts = blocks.experts
    meta_width = blocks.columns
    count = len(offsets) * size
    terms = [term for piece in pieces for term in piece]
    layout = (segments, [len(piece) for piece in pieces], len(arrays), places)
    kinds = len(pieces[0])
    scratch = [
        pltpu.VMEM((kinds, 3, count, hidden), bf16),
        pltpu.VMEM((count, meta_width), bf16),
        pltpu.SemaphoreType.DMA((kinds * len(segments) + len(places),)),
    ]
    parities = [r % 2 for r in offsets]
    columns = 2 * width + (2 * experts + 127) // 128 * 128
    halves = [shape(parities.count(p) * size, columns) for p in (0, 1) if parities.count(p)]
    return pl.pallas_call(
        functools.partial(expert_kernel, layout, experts, parities),
        in_specs=[IN_SMEM] + [IN_ANY] * (len(terms) + len(arrays)) + [IN_VMEM] * 3,
        out_specs=[IN_VMEM] * (3 + len(halves)),
        out_shape=[shape(count, hidden)] * 3 + halves,
        scratch_shapes=scratch,
        compiler_params=grant(ROOM if count <= 256 else 2 * ROOM),
        cost_estimate=cost(),
        name="expert_rows",
    )(me, tie(terms[0], *after), *terms[1:], *arrays, *plain)


def gradient_kernel(layout, *refs):
    places, column, sizes, count, before, ends, far = layout
    chunks, data = refs[: len(sizes)], refs[len(sizes) :][:count]
    earlier = refs[len(sizes) + count] if before else None
    out = refs[len(sizes) + count + before]
    rows, delta, tiles, sems, out_sems = refs[len(sizes) + count + before + 1 :][:5]
    size, width = data[0].shape[1], rows.shape[1]
    if far:
        held, held_sem = refs[-2:]
        held_copy = pltpu.make_async_copy(earlier, held, held_sem)
        earlier = held
    pairs = []
    for i, (a, j) in enumerate(places):
        pairs.append((data[a].at[j, :, pl.ds(column, width)], rows.at[pl.ds(i * size, size)]))
    start = 0
    for ref, many in zip(chunks, sizes):
        pairs.append((ref, delta.at[pl.ds(start, many)]))
        start += many
    copies = [pltpu.make_async_copy(*pair, sems.at[i]) for i, pair in enumerate(pairs)]
    for copy in copies:
        copy.start()
    if far:
        held_copy.start()
    for copy in copies:
        copy.wait()
    if far:
        held_copy.wait()
    sent = []
    for k in range(delta.shape[1] // STEP):
        here = slice(k * STEP, (k + 1) * STEP)
        value = first_first(delta[:, here], rows[...])
        if before:
            value = value + earlier[here, :].astype(f32)
        if not ends:
            out[here, :] = value.astype(bf16)
            continue
        slot = k % tiles.shape[0]
        if k >= tiles.shape[0]:
            sent[k - tiles.shape[0]].wait()
        tiles[slot] = value.astype(bf16)
        copy = pltpu.make_async_copy(tiles.at[slot], out.at[pl.ds(k * STEP, STEP)], out_sems.at[k])
        copy.start()
        sent.append(copy)
    for copy in sent[-tiles.shape[0] :]:
        copy.wait()


def weight_gradient(blocks, offsets, chunks, column, before, ends, far, after):
    arrays, places = blocks.use(offsets)
    hidden = chunks[0].shape[1]
    width = (arrays[0].shape[2] - blocks.columns) // 2
    sizes = [d.shape[0] for d in chunks]
    steps = hidden // STEP
    earlier = [] if before is None else [before]
    out_far = ends or (far and before is None)
    in_far = far and before is not None
    layout = (places, column * width, sizes, len(arrays), len(earlier), out_far, in_far)
    return pl.pallas_call(
        functools.partial(gradient_kernel, layout),
        in_specs=[IN_ANY] * (len(chunks) + len(arrays)) + [IN_ANY if far else IN_VMEM] * len(earlier),
        out_specs=IN_ANY if out_far else IN_VMEM,
        out_shape=shape(hidden, width) if out_far else pltpu.VMEM((hidden, width), bf16),
        scratch_shapes=[
            pltpu.VMEM((sum(sizes), width), bf16),
            pltpu.VMEM((sum(sizes), hidden), bf16),
            pltpu.VMEM((3 if out_far else 1, STEP, width), bf16),
            pltpu.SemaphoreType.DMA((len(places) + len(chunks),)),
            pltpu.SemaphoreType.DMA((steps,)),
        ]
        + [pltpu.VMEM((hidden, width), bf16), pltpu.SemaphoreType.DMA(())] * in_far,
        compiler_params=grant(16 if in_far else 10),
        cost_estimate=cost(),
        name="weight_gradient",
    )(tie(chunks[0], *after), *chunks[1:], *arrays, *earlier)


def swap(part):
    if lax.axis_size("dp") == 2:
        return [part, lax.ppermute(part, "dp", [(0, 1), (1, 0)])]
    return [lax.psum(part, "dp")]


def add_kernel(spans, left, right, *outs):
    for (left_row, right_row), out in zip(spans, outs):
        count = out.shape[0]
        total = left[left_row : left_row + count].astype(f32) + right[right_row : right_row + count].astype(f32)
        out[...] = total.astype(bf16)


def add_rows(left, right, spans, rows):
    return pl.pallas_call(
        functools.partial(add_kernel, spans),
        out_shape=[shape(rows, left.shape[1])] * len(spans),
        compiler_params=grant(ROOM),
        cost_estimate=cost(),
        name="add_rows",
    )(left, right)


def final_kernel(experts, payload, *refs):
    terms, (out, grad, route, meta, sem) = refs[:-5], refs[-5:]
    width, lanes = out.shape[1], meta.shape[1]
    copy = pltpu.make_async_copy(payload.at[0, :, pl.ds(payload.shape[2] - lanes, lanes)], meta, sem)
    copy.start()

    def total(here):
        value = terms[0][:, here].astype(f32)
        for term in terms[1:]:
            value = value + term[:, here].astype(f32)
        return value

    out[...] = total(slice(0, width)).astype(bf16)
    grad[...] = total(slice(width, 2 * width)).astype(bf16)
    table = total(slice(2 * width, terms[0].shape[1]))
    copy.wait()
    lane = lax.broadcasted_iota(jnp.int32, table.shape, 1)
    found = jnp.zeros(table.shape, f32)
    for k in range(route.shape[0]):
        wanted = meta[:, 3 * experts + k : 3 * experts + k + 1].astype(jnp.int32)
        mine = (lane == wanted) | (lane == wanted + experts)
        value = jnp.sum(jnp.where(mine, table, 0.0), axis=1, keepdims=True)
        found = jnp.where(lane == k, value, found)
    route[...] = found.T[: route.shape[0]]


def final_sums(payload, terms, width, chosen, experts, lanes):
    rows = payload.shape[1]
    return pl.pallas_call(
        functools.partial(final_kernel, experts),
        in_specs=[IN_ANY] + [IN_VMEM] * len(terms),
        out_shape=[shape(rows, width)] * 2 + [shape(chosen, rows, dtype=f32)],
        scratch_shapes=[pltpu.VMEM((rows, lanes), bf16), pltpu.SemaphoreType.DMA(())],
        compiler_params=grant(ROOM),
        cost_estimate=cost(),
        name="final_sums",
    )(payload, *terms)


def local(tokens, expert_ids, route_weights, gate_weight, up_weight, down_weight, output_grad):
    experts = lax.axis_size("expert")
    rows, width = tokens.shape
    me = lax.axis_index("expert").astype(jnp.int32).reshape(1)
    weights = [gate_weight[0], up_weight[0], down_weight[0]]
    columns = weight_columns(expert_ids, route_weights, experts)
    lanes = columns.shape[1]
    payload = tie(jnp.concatenate([tokens, output_grad, columns], axis=1)[None], me)

    def both(evens):
        return list(evens) + [e + 1 for e in evens]

    half = experts // 2
    first = [half]
    stages, held = [], [0, half]
    for bit in [1 << i for i in reversed(range(2, half.bit_length() - 1))]:
        stages.append([r ^ bit for r in held])
        held = held + stages[-1]
    early = [r for stage in stages for r in stage]
    if len(stages) == 1:
        near, far = sorted(early)
        lead, groups = [far], [[far, far ^ 2], [near, half ^ 2], [near ^ 2, 2]]
    else:
        lead, size = stages[0], experts // 8
        rest = [r for r in early if r not in lead] + [r ^ 2 for r in first + early] + [2]
        groups = [lead] + [rest[i : i + size] for i in range(0, len(rest), size)]
    rest = [r for group in groups for r in group if r not in lead]

    blocks = Blocks(payload, experts, lanes)
    blocks.cores([0])
    blocks.fetch(half, first)
    blocks.fetch(2, [2])
    if len(stages) == 1:
        blocks.fetch(near, [near])
    part, plain = load_weights(blocks, [0, 1], weights)
    blocks.cores(first, after=[part] + blocks.arrays[2:])
    if len(stages) == 1:
        blocks.fetch(near, [far], after=[part])
    else:
        known = [0] + first
        for stage in stages:
            blocks.join(known)
            blocks.fetch(stage[0] ^ known[0], stage)
            known = known + stage
    blocks.fetch(2, [half ^ 2], after=[part])
    gate = blocks.arrays[-1:]
    if len(stages) == 1:
        blocks.fetch(2, [near ^ 2], after=[part])
        gate = blocks.arrays[-2:]

    clock = [0]
    after = [part]
    dues = []

    def step(kernel, *arguments, **options):
        clock[0] += 1
        now = [value for due, value in dues if due <= clock[0]]
        dues[:] = [each for each in dues if each[0] > clock[0]]
        made = kernel(*arguments, after=after + now, **options)
        after[:] = [made[0] if isinstance(made, (list, tuple)) else made]
        return made

    pieces, lines = [], {}

    def send(made, offsets, piece):
        pieces.append(swap(made))
        base = 0
        for start, stop, m in piece:
            for r in offsets[start:stop]:
                lines[(r, m)] = (len(pieces) - 1, base)
                base += rows

    def whole(start, stop):
        return [(start, stop, m) for m in range(3)]

    def products(offsets, *wanted):
        wanted = wanted or (whole(0, len(offsets)),)
        for made, piece in zip(step(partial_products, blocks, offsets, wanted, plain), wanted):
            send(made, offsets, piece)

    def terms_of(offsets):
        found, used = [], []
        for m in range(3):
            for i, r in enumerate(offsets):
                piece, row = lines[(r, m)]
                if piece not in used:
                    used.append(piece)
                last = found[-1] if found else None
                if last and (last[0], last[3], last[4] + last[2]) == (m, used.index(piece), row):
                    last[2] += rows
                else:
                    found.append([m, i * rows, rows, used.index(piece), row])
        return tuple(tuple(line) for line in found), [pieces[p] for p in used]

    results, returned, summed = [], [], []

    def expert_rows(evens, core_due=None, due=None, gate=(), send_gate=()):
        offsets = both(evens)
        act, gate_delta, up_delta, even, odd = step(
            expert_call, blocks, offsets, *terms_of(offsets), plain, me
        )
        results.append((act, gate_delta, up_delta))
        spans = [(i * rows, i * rows) for i in range(len(evens))]
        sums = add_rows(even, flip(tie(odd, *gate), 1), spans, rows)
        if core_due:
            dues.append((clock[0] + core_due, sums[0]))
        for r, value in zip(evens, sums):
            if r:
                value = flip(tie(value, *send_gate), r)
                if due:
                    dues.append((clock[0] + due, value))
            returned.append(value)

    def arrived(piece):
        return pieces[piece][1:]

    def arrived(piece):
        return pieces[piece][1:]

    def halves(start, stop):
        middle = (start + stop + 1) // 2
        return [whole(start, middle), whole(middle, stop)]

    send(part, [0, 1], whole(0, 2))
    products(both(first))
    for run in [[far]] if len(stages) == 1 else stages:
        blocks.fetch(2, [r ^ 2 for r in run], after=arrived(0))
    blocks.cores(lead, after=gate)

    def paired(evens):
        return [r for e in evens for r in (e, e + 1)]

    products(paired(lead))
    blocks.join(rest, after=after)
    blocks.cores(rest, after=arrived(1))
    wanted, leads, at = [], [], 0
    for group in groups:
        group = [r for r in group if r not in lead]
        leads.append(3 + len(wanted))
        if len(group) > 1:
            wanted += halves(at, at + 2 * len(group))
        elif group:
            wanted.append(whole(at, at + 2 * len(group)))
        at += 2 * len(group)
    expert_rows([0] + first, due=2, send_gate=arrived(2))
    products(paired(rest), *wanted)
    worked = both([0] + first)
    gradients = [None] * 3

    def add_gradients(offsets, chunks_from, kinds, ends):
        for kind in kinds:
            chunks = [done[kind] for done in results[chunks_from:]]
            gradients[kind] = step(
                weight_gradient, blocks, offsets, chunks, int(kind == 0), gradients[kind], ends, kind == 0
            )

    for i, group in enumerate(groups):
        left = len(groups) - 1 - i
        if left == 1:
            add_gradients(worked, 0, (0, 1, 2), False)
            summed_rows, summed_chunks = len(worked), len(results)
        if left == 0:
            expert_rows(group, core_due=1, gate=sent)
        else:
            gate = arrived(leads[i + 1]) + (sent if left == 1 else [])
            expert_rows(group, core_due=1 if left == 1 else None, gate=gate)
            sent = returned[-len(group) :]
        worked = worked + both(group)
    add_gradients(worked[summed_rows:], summed_chunks, (1, 2, 0), True)
    down_gradient, gate_gradient, up_gradient = gradients
    layer_output, token_gradient, route_gradient = final_sums(
        payload, returned, width, expert_ids.shape[1], experts, lanes
    )
    return (
        layer_output,
        token_gradient,
        route_gradient.T,
        gate_gradient[None],
        up_gradient[None],
        down_gradient[None],
    )


def solution(mesh):
    by_token = P("expert", "dp")
    by_row = P("expert", None)
    by_weight = P("expert", None, "dp")
    return jax.shard_map(
        local,
        mesh=mesh,
        in_specs=(by_token, by_row, by_row, by_weight, by_weight, by_weight, by_token),
        out_specs=(by_token, by_token, by_row, by_weight, by_weight, by_weight),
        check_vma=False,
    )
```

```python
import functools
import jax
import jax.numpy as jnp
from jax import lax
from jax.experimental import pallas as pl
from jax.experimental.pallas import tpu as pltpu
from jax.sharding import PartitionSpec as P

f32 = jnp.float32
bf16 = jnp.bfloat16
STEP = 256
ROOM = 12
IN_VMEM = pl.BlockSpec(memory_space=pltpu.VMEM)
IN_HBM = pl.BlockSpec(memory_space=pltpu.HBM)
IN_ANY = pl.BlockSpec(memory_space=pl.ANY)
IN_SMEM = pl.BlockSpec(memory_space=pltpu.SMEM)


def grant(mebibytes):
    return pltpu.CompilerParams(vmem_limit_bytes=mebibytes << 20)


def cost(flops=1 << 28):
    return pl.CostEstimate(flops=flops, bytes_accessed=1, transcendentals=0)


def tie(value, *earlier):
    return lax.optimization_barrier((value, *earlier))[0]


def shape(*dims, dtype=bf16):
    return jax.ShapeDtypeStruct(dims, dtype)


def flip(block, bit):
    count = lax.axis_size("expert")
    return lax.ppermute(block, "expert", [(i, i ^ bit) for i in range(count)])


def lowest_bit(number):
    return number & -number


def bits_of(number):
    return bin(number).count("1")


def split_bf16(value, pieces):
    out = []
    for _ in range(pieces):
        head = lax.reduce_precision(value, 8, 7)
        out.append(head.astype(bf16))
        value = value - head
    return out


def matmul(lhs, rhs):
    return lax.dot_general(lhs, rhs, (((1,), (0,)), ((), ())), preferred_element_type=f32)


def last_last(lhs, rhs):
    return lax.dot_general(lhs, rhs, (((1,), (1,)), ((), ())), preferred_element_type=f32)


def first_first(lhs, rhs):
    return lax.dot_general(lhs, rhs, (((0,), (0,)), ((), ())), preferred_element_type=f32)


def weight_columns(expert_ids, route_weights, experts):
    hit = expert_ids[:, :, None] == jnp.arange(experts, dtype=jnp.int32)[None, None, :]
    table = jnp.sum(jnp.where(hit, route_weights[:, :, None], 0.0), axis=1)
    columns = jnp.concatenate(split_bf16(table, 3) + [expert_ids.astype(bf16)], axis=1)
    return jnp.pad(columns, ((0, 0), (0, -columns.shape[1] % 128)))


class Blocks:
    def __init__(self, payload, experts, columns):
        self.arrays, self.place = [payload], {0: (0, 0)}
        self.experts, self.columns = experts, columns

    def add(self, array, offsets):
        self.arrays.append(array)
        for i, r in enumerate(offsets):
            self.place[r] = (len(self.arrays) - 1, i)

    def fetch(self, bit, offsets, after=()):
        array = self.joined([r ^ bit for r in offsets])
        self.add(flip(tie(array, *after), bit), offsets)

    def cores(self, evens, after=()):
        self.add(flip(tie(self.joined(evens), *after), 1), [r + 1 for r in evens])

    def joined(self, offsets):
        if offsets == [0]:
            return self.arrays[0]
        places = [self.place[r] for r in offsets]
        array = self.arrays[places[0][0]]
        if places == [(places[0][0], i) for i in range(array.shape[0])]:
            return array
        return jnp.concatenate([self.arrays[a][i : i + 1] for a, i in places], axis=0)

    def join(self, offsets, after=()):
        arrays, places = self.use(offsets)
        made = pl.pallas_call(
            functools.partial(join_kernel, places),
            in_specs=[IN_ANY] * len(arrays),
            out_specs=IN_ANY,
            out_shape=shape(len(offsets), *arrays[0].shape[1:]),
            scratch_shapes=[pltpu.SemaphoreType.DMA((len(offsets),))],
            compiler_params=grant(ROOM),
            cost_estimate=cost(),
            name="join_blocks",
        )(tie(arrays[0], *after), *arrays[1:])
        self.add(made, offsets)
        return made

    def use(self, offsets):
        needed = sorted({self.place[r][0] for r in offsets})
        return [self.arrays[a] for a in needed], [
            (needed.index(self.place[r][0]), self.place[r][1]) for r in offsets
        ]


def join_kernel(places, *refs):
    data, out, sems = refs[:-2], refs[-2], refs[-1]
    copies = [pltpu.make_async_copy(data[a].at[j], out.at[i], sems.at[i]) for i, (a, j) in enumerate(places)]
    for copy in copies:
        copy.start()
    for copy in copies:
        copy.wait()


def load_kernel(places, count, *refs):
    data, sources, part = refs[:count], refs[count : count + 3], refs[count + 3]
    kept, (rows, sems, row_sems) = refs[count + 4 : count + 7], refs[-3:]
    size, width = data[0].shape[1], rows.shape[2]
    steps = sems.shape[1]
    many, total = sources[0].shape[0] // steps, rows.shape[1]
    row_copies = [
        pltpu.make_async_copy(
            data[a].at[j, :, pl.ds(source * width, width)],
            rows.at[source, pl.ds(i * size, size)],
            row_sems.at[source, i],
        )
        for source in range(2)
        for i, (a, j) in enumerate(places)
    ]
    copies = {}
    for m in range(3):
        for t in range(steps):
            here = pl.ds(t * many, many)
            copies[m, t] = pltpu.make_async_copy(sources[m].at[here], kept[m].at[here], sems.at[m, t])
    for each in row_copies:
        each.start()
    for each in copies.values():
        each.start()
    for each in row_copies:
        each.wait()
    for m in range(3):
        for t in range(steps):
            copies[m, t].wait()
            here = slice(t * many, (t + 1) * many)
            part[m * total : (m + 1) * total, here] = last_last(rows[int(m == 2)], kept[m][here, :]).astype(bf16)


def load_weights(blocks, offsets, weights):
    arrays, places = blocks.use(offsets)
    hidden, width = weights[0].shape
    count = len(offsets) * arrays[0].shape[1]
    out = pl.pallas_call(
        functools.partial(load_kernel, places, len(arrays)),
        in_specs=[IN_ANY] * (len(arrays) + 3),
        out_specs=[IN_VMEM] * 4,
        out_shape=[shape(3 * count, hidden)] + [pltpu.VMEM((hidden, width), bf16)] * 3,
        scratch_shapes=[
            pltpu.VMEM((2, count, width), bf16),
            pltpu.SemaphoreType.DMA((3, 3)),
            pltpu.SemaphoreType.DMA((2, len(offsets))),
        ],
        compiler_params=grant(34),
        cost_estimate=cost(),
        name="load_weights",
    )(*arrays, *weights)
    return out[0], out[1:]


def part_kernel(places, pieces, count, *refs):
    data, weights = refs[:count], refs[count : count + 3]
    parts, (rows, sems) = refs[count + 3 : -2], refs[-2:]
    size, width = data[0].shape[1], rows.shape[2]
    copies = {}
    for source in range(2):
        for i, (a, j) in enumerate(places):
            copies[source, i] = pltpu.make_async_copy(
                data[a].at[j, :, pl.ds(source * width, width)],
                rows.at[source, pl.ds(i * size, size)],
                sems.at[source, i],
            )
    for copy in copies.values():
        copy.start()
    for m in range(3):
        wanted = [
            (part, each) for part, piece in zip(parts, pieces) for each in piece if each[2] == m
        ]
        if m != 1:
            for i in range(len(places)):
                copies[int(m == 2), i].wait()
        if not wanted:
            continue
        low = min(each[0] for _, each in wanted)
        high = max(each[1] for _, each in wanted)
        value = last_last(rows[int(m == 2), low:high], weights[m][...]).astype(bf16)
        for part, (start, stop, _, base) in wanted:
            part[base : base + stop - start] = value[start - low : stop - low]


def partial_products(blocks, offsets, pieces, weights, after):
    arrays, places = blocks.use(offsets)
    size = arrays[0].shape[1]
    hidden, width = weights[0].shape
    count = len(offsets) * size
    spans, heights = [], []
    for piece in pieces:
        lines, base = [], 0
        for start, stop, m in piece:
            lines.append((start * size, stop * size, m, base))
            base += (stop - start) * size
        spans.append(lines)
        heights.append(base)
    return pl.pallas_call(
        functools.partial(part_kernel, places, spans, len(arrays)),
        in_specs=[IN_ANY] * len(arrays) + [IN_VMEM] * 3,
        out_specs=[IN_VMEM] * len(pieces),
        out_shape=[shape(height, hidden) for height in heights],
        scratch_shapes=[
            pltpu.VMEM((2, count, width), bf16),
            pltpu.SemaphoreType.DMA((2, len(offsets))),
        ],
        compiler_params=grant(ROOM if count <= 320 else 2 * ROOM),
        cost_estimate=cost(),
        name="partial_products",
    )(tie(arrays[0], *after), *arrays[1:], *weights)


def fetch_terms(layout, refs, terms, meta, sems):
    segments, counts, count, places = layout
    pieces, at = [], 0
    for n in counts:
        pieces.append(refs[at : at + n])
        at += n
    data = refs[at : at + count]
    pairs = []
    for m, start, rows, p, p_row in segments:
        for i, ref in enumerate(pieces[p]):
            pairs.append((ref.at[pl.ds(p_row, rows)], terms.at[i, m, pl.ds(start, rows)]))
    size, columns = data[0].shape[1], data[0].shape[2]
    for i, (a, j) in enumerate(places):
        pairs.append(
            (
                data[a].at[j, :, pl.ds(columns - meta.shape[1], meta.shape[1])],
                meta.at[pl.ds(i * size, size)],
            )
        )
    copies = [pltpu.make_async_copy(*pair, sems.at[i]) for i, pair in enumerate(pairs)]
    for copy in copies:
        copy.start()
    return copies


def own_weight(meta, experts, me):
    lane = lax.broadcasted_iota(jnp.int32, meta.shape, 1)
    mine = (lane == me) | (lane == me + experts) | (lane == me + 2 * experts)
    return jnp.sum(jnp.where(mine, meta[...].astype(f32), 0.0), axis=1, keepdims=True)


def expert_kernel(layout, experts, parities, me_ref, *refs):
    segments, counts, count, places = layout
    inputs = sum(counts) + count
    gate, up, down, act, gate_delta, up_delta = refs[inputs : inputs + 6]
    results, (terms, meta, sems) = refs[inputs + 6 : -3], refs[-3:]
    for copy in fetch_terms(layout, refs[:inputs], terms, meta, sems):
        copy.wait()
    width = down.shape[1]
    size = meta.shape[0] // len(parities)
    me = me_ref[0]
    weight = own_weight(meta, experts, me)
    route = jnp.zeros(weight.shape, f32)
    for t in range(act.shape[1] // STEP):
        here = slice(t * STEP, (t + 1) * STEP)
        total = terms[0, :, :, here].astype(f32)
        for i in range(1, terms.shape[0]):
            total = total + terms[i, :, :, here].astype(f32)
        gate_pre, up_pre, raw_grad = total[0], total[1], total[2]
        sigmoid_gate = jax.nn.sigmoid(gate_pre)
        silu_gate = gate_pre * sigmoid_gate
        product = silu_gate * up_pre
        hidden_grad = raw_grad * weight
        slope = sigmoid_gate * (1.0 + gate_pre * (1.0 - sigmoid_gate))
        act[:, here] = (product * weight).astype(bf16)
        gate_delta[:, here] = (hidden_grad * up_pre * slope).astype(bf16)
        up_delta[:, here] = (hidden_grad * silu_gate).astype(bf16)
        route = route + jnp.sum(product * raw_grad, axis=1, keepdims=True)

    def store(here, value):
        used = [0, 0]
        for i, odd in enumerate(parities):
            results[odd if len(results) > 1 else 0][used[odd] : used[odd] + size, here] = value[
                i * size : (i + 1) * size
            ]
            used[odd] += size

    tile = min(512, width)
    for t in range(width // tile):
        here = slice(t * tile, (t + 1) * tile)
        store(here, matmul(act[...], down[:, here]).astype(bf16))
        value = matmul(gate_delta[...], gate[:, here]) + matmul(up_delta[...], up[:, here])
        store(slice(width + t * tile, width + (t + 1) * tile), value.astype(bf16))
    columns = results[0].shape[1]
    lane = lax.broadcasted_iota(jnp.int32, (weight.shape[0], columns - 2 * width), 1)
    head = route.astype(bf16).astype(f32)
    spread = jnp.where(lane == me, head, jnp.where(lane == me + experts, route - head, 0.0))
    store(slice(2 * width, columns), spread.astype(bf16))


def expert_call(blocks, offsets, segments, pieces, plain, me, after):
    arrays, places = blocks.use(offsets)
    size = arrays[0].shape[1]
    hidden, width = plain[0].shape
    experts = blocks.experts
    meta_width = blocks.columns
    count = len(offsets) * size
    terms = [term for piece in pieces for term in piece]
    layout = (segments, [len(piece) for piece in pieces], len(arrays), places)
    kinds = len(pieces[0])
    scratch = [
        pltpu.VMEM((kinds, 3, count, hidden), bf16),
        pltpu.VMEM((count, meta_width), bf16),
        pltpu.SemaphoreType.DMA((kinds * len(segments) + len(places),)),
    ]
    parities = [r % 2 for r in offsets]
    columns = 2 * width + (2 * experts + 127) // 128 * 128
    halves = [shape(parities.count(p) * size, columns) for p in (0, 1) if parities.count(p)]
    return pl.pallas_call(
        functools.partial(expert_kernel, layout, experts, parities),
        in_specs=[IN_SMEM] + [IN_ANY] * (len(terms) + len(arrays)) + [IN_VMEM] * 3,
        out_specs=[IN_VMEM] * (3 + len(halves)),
        out_shape=[shape(count, hidden)] * 3 + halves,
        scratch_shapes=scratch,
        compiler_params=grant(ROOM if count <= 256 else 2 * ROOM),
        cost_estimate=cost(),
        name="expert_rows",
    )(me, tie(terms[0], *after), *terms[1:], *arrays, *plain)


def gradient_kernel(layout, *refs):
    places, column, sizes, count, kinds, before, ends, far = layout
    n = kinds * len(sizes)
    chunks, data = refs[:n], refs[n:][:count]
    earlier = refs[n + count :][: kinds * before]
    outs = refs[n + count + kinds * before :][:kinds]
    rows, delta, tiles, sems, out_sems = refs[n + count + kinds * before + kinds :][:5]
    size, width = data[0].shape[1], rows.shape[1]
    if far:
        held, held_sem = refs[-2:]
        held_copy = pltpu.make_async_copy(earlier[0], held, held_sem)
        earlier = [held]
    pairs = []
    for i, (a, j) in enumerate(places):
        pairs.append((0, data[a].at[j, :, pl.ds(column, width)], rows.at[pl.ds(i * size, size)]))
    for kind in range(kinds):
        start = 0
        for i, many in enumerate(sizes):
            pairs.append((kind, chunks[kind * len(sizes) + i], delta.at[kind, pl.ds(start, many)]))
            start += many
    copies = [(kind, pltpu.make_async_copy(*pair, sems.at[i])) for i, (kind, *pair) in enumerate(pairs)]
    for _, copy in copies:
        copy.start()
    if far:
        held_copy.start()
    sent = []
    for kind in range(kinds):
        for owner, copy in copies:
            if owner == kind:
                copy.wait()
        if far:
            held_copy.wait()
        for k in range(delta.shape[2] // STEP):
            here = slice(k * STEP, (k + 1) * STEP)
            value = first_first(delta[kind, :, here], rows[...])
            if before:
                value = value + earlier[kind][here, :].astype(f32)
            if not ends:
                outs[kind][here, :] = value.astype(bf16)
                continue
            at = len(sent)
            slot = at % tiles.shape[0]
            if at >= tiles.shape[0]:
                sent[at - tiles.shape[0]].wait()
            tiles[slot] = value.astype(bf16)
            copy = pltpu.make_async_copy(
                tiles.at[slot], outs[kind].at[pl.ds(k * STEP, STEP)], out_sems.at[at]
            )
            copy.start()
            sent.append(copy)
    for copy in sent[-tiles.shape[0] :]:
        copy.wait()


def weight_gradients(blocks, offsets, deltas, column, before, ends, far, after):
    arrays, places = blocks.use(offsets)
    hidden = deltas[0][0].shape[1]
    width = (arrays[0].shape[2] - blocks.columns) // 2
    sizes = [d.shape[0] for d in deltas[0]]
    kinds, steps = len(deltas), hidden // STEP
    chunks = [d for delta in deltas for d in delta]
    out_far = ends or (far and not before)
    in_far = far and bool(before)
    layout = (places, column * width, sizes, len(arrays), kinds, bool(before), out_far, in_far)
    return pl.pallas_call(
        functools.partial(gradient_kernel, layout),
        in_specs=[IN_ANY] * (len(chunks) + len(arrays)) + [IN_ANY if far else IN_VMEM] * len(before),
        out_specs=[IN_ANY if out_far else IN_VMEM] * kinds,
        out_shape=[shape(hidden, width) if out_far else pltpu.VMEM((hidden, width), bf16)] * kinds,
        scratch_shapes=[
            pltpu.VMEM((sum(sizes), width), bf16),
            pltpu.VMEM((kinds, sum(sizes), hidden), bf16),
            pltpu.VMEM((4 if out_far else 1, STEP, width), bf16),
            pltpu.SemaphoreType.DMA((len(places) + len(chunks),)),
            pltpu.SemaphoreType.DMA((kinds * steps,)),
        ]
        + [pltpu.VMEM((hidden, width), bf16), pltpu.SemaphoreType.DMA(())] * in_far,
        compiler_params=grant(16 if in_far else 10 if kinds == 1 else 12),
        cost_estimate=cost(),
        name="weight_gradients",
    )(tie(chunks[0], *after), *chunks[1:], *arrays, *before)


def swap(part):
    if lax.axis_size("dp") == 2:
        return [part, lax.ppermute(part, "dp", [(0, 1), (1, 0)])]
    return [lax.psum(part, "dp")]


def add_kernel(spans, left, right, *outs):
    for (left_row, right_row), out in zip(spans, outs):
        count = out.shape[0]
        total = left[left_row : left_row + count].astype(f32) + right[right_row : right_row + count].astype(f32)
        out[...] = total.astype(bf16)


def add_rows(left, right, spans, rows):
    return pl.pallas_call(
        functools.partial(add_kernel, spans),
        out_shape=[shape(rows, left.shape[1])] * len(spans),
        compiler_params=grant(ROOM),
        cost_estimate=cost(),
        name="add_rows",
    )(left, right)


def final_kernel(experts, payload, *refs):
    terms, (out, grad, route, meta, sem) = refs[:-5], refs[-5:]
    width, lanes = out.shape[1], meta.shape[1]
    copy = pltpu.make_async_copy(payload.at[0, :, pl.ds(payload.shape[2] - lanes, lanes)], meta, sem)
    copy.start()

    def total(here):
        value = terms[0][:, here].astype(f32)
        for term in terms[1:]:
            value = value + term[:, here].astype(f32)
        return value

    out[...] = total(slice(0, width)).astype(bf16)
    grad[...] = total(slice(width, 2 * width)).astype(bf16)
    table = total(slice(2 * width, terms[0].shape[1]))
    copy.wait()
    lane = lax.broadcasted_iota(jnp.int32, table.shape, 1)
    found = jnp.zeros(table.shape, f32)
    for k in range(route.shape[0]):
        wanted = meta[:, 3 * experts + k : 3 * experts + k + 1].astype(jnp.int32)
        mine = (lane == wanted) | (lane == wanted + experts)
        value = jnp.sum(jnp.where(mine, table, 0.0), axis=1, keepdims=True)
        found = jnp.where(lane == k, value, found)
    route[...] = found.T[: route.shape[0]]


def final_sums(payload, terms, width, chosen, experts, lanes):
    rows = payload.shape[1]
    return pl.pallas_call(
        functools.partial(final_kernel, experts),
        in_specs=[IN_ANY] + [IN_VMEM] * len(terms),
        out_shape=[shape(rows, width)] * 2 + [shape(chosen, rows, dtype=f32)],
        scratch_shapes=[pltpu.VMEM((rows, lanes), bf16), pltpu.SemaphoreType.DMA(())],
        compiler_params=grant(ROOM),
        cost_estimate=cost(),
        name="final_sums",
    )(payload, *terms)


def local(tokens, expert_ids, route_weights, gate_weight, up_weight, down_weight, output_grad):
    experts = lax.axis_size("expert")
    rows, width = tokens.shape
    me = lax.axis_index("expert").astype(jnp.int32).reshape(1)
    weights = [gate_weight[0], up_weight[0], down_weight[0]]
    columns = weight_columns(expert_ids, route_weights, experts)
    lanes = columns.shape[1]
    payload = tie(jnp.concatenate([tokens, output_grad, columns], axis=1)[None], me)

    def both(evens):
        return list(evens) + [e + 1 for e in evens]

    half = experts // 2
    first = [half]
    stages, held = [], [0, half]
    for bit in [1 << i for i in reversed(range(2, half.bit_length() - 1))]:
        stages.append([r ^ bit for r in held])
        held = held + stages[-1]
    early = [r for stage in stages for r in stage]
    if len(stages) == 1:
        near, far = sorted(early)
        lead, groups = [far], [[far, far ^ 2], [near, half ^ 2], [near ^ 2, 2]]
    else:
        lead, size = stages[0], experts // 8
        rest = [r for r in early if r not in lead] + [r ^ 2 for r in first + early] + [2]
        groups = [lead] + [rest[i : i + size] for i in range(0, len(rest), size)]
    rest = [r for group in groups for r in group if r not in lead]

    blocks = Blocks(payload, experts, lanes)
    blocks.cores([0])
    blocks.fetch(half, first)
    blocks.fetch(2, [2])
    if len(stages) == 1:
        blocks.fetch(near, [near])
    part, plain = load_weights(blocks, [0, 1], weights)
    blocks.cores(first, after=[part] + blocks.arrays[2:])
    if len(stages) == 1:
        blocks.fetch(near, [far], after=[part])
    else:
        known = [0] + first
        for stage in stages:
            blocks.join(known)
            blocks.fetch(stage[0] ^ known[0], stage)
            known = known + stage
    blocks.fetch(2, [half ^ 2], after=[part])
    gate = blocks.arrays[-1:]
    if len(stages) == 1:
        blocks.fetch(2, [near ^ 2], after=[part])
        gate = blocks.arrays[-2:]

    clock = [0]
    after = [part]
    dues = []

    def step(kernel, *arguments, **options):
        clock[0] += 1
        now = [value for due, value in dues if due <= clock[0]]
        dues[:] = [each for each in dues if each[0] > clock[0]]
        made = kernel(*arguments, after=after + now, **options)
        after[:] = [made[0] if isinstance(made, (list, tuple)) else made]
        return made

    pieces, lines = [], {}

    def send(made, offsets, piece):
        pieces.append(swap(made))
        base = 0
        for start, stop, m in piece:
            for r in offsets[start:stop]:
                lines[(r, m)] = (len(pieces) - 1, base)
                base += rows

    def whole(start, stop):
        return [(start, stop, m) for m in range(3)]

    def products(offsets, *wanted):
        wanted = wanted or (whole(0, len(offsets)),)
        for made, piece in zip(step(partial_products, blocks, offsets, wanted, plain), wanted):
            send(made, offsets, piece)

    def terms_of(offsets):
        found, used = [], []
        for m in range(3):
            for i, r in enumerate(offsets):
                piece, row = lines[(r, m)]
                if piece not in used:
                    used.append(piece)
                last = found[-1] if found else None
                if last and (last[0], last[3], last[4] + last[2]) == (m, used.index(piece), row):
                    last[2] += rows
                else:
                    found.append([m, i * rows, rows, used.index(piece), row])
        return tuple(tuple(line) for line in found), [pieces[p] for p in used]

    results, returned, summed = [], [], []

    def expert_rows(evens, core_due=None, due=None, gate=(), send_gate=()):
        offsets = both(evens)
        act, gate_delta, up_delta, even, odd = step(
            expert_call, blocks, offsets, *terms_of(offsets), plain, me
        )
        results.append((act, gate_delta, up_delta))
        spans = [(i * rows, i * rows) for i in range(len(evens))]
        sums = add_rows(even, flip(tie(odd, *gate), 1), spans, rows)
        if core_due:
            dues.append((clock[0] + core_due, sums[0]))
        for r, value in zip(evens, sums):
            if r:
                value = flip(tie(value, *send_gate), r)
                if due:
                    dues.append((clock[0] + due, value))
            returned.append(value)

    def arrived(piece):
        return pieces[piece][1:]

    def arrived(piece):
        return pieces[piece][1:]

    def halves(start, stop):
        middle = (start + stop + 1) // 2
        return [whole(start, middle), whole(middle, stop)]

    send(part, [0, 1], whole(0, 2))
    products(both(first))
    for run in [[far]] if len(stages) == 1 else stages:
        blocks.fetch(2, [r ^ 2 for r in run], after=arrived(0))
    blocks.cores(lead, after=gate)

    def paired(evens):
        return [r for e in evens for r in (e, e + 1)]

    products(paired(lead))
    blocks.join(rest, after=after)
    blocks.cores(rest, after=arrived(1))
    wanted, leads, at = [], [], 0
    for group in groups:
        group = [r for r in group if r not in lead]
        leads.append(3 + len(wanted))
        if len(group) > 1:
            wanted += halves(at, at + 2 * len(group))
        elif group:
            wanted.append(whole(at, at + 2 * len(group)))
        at += 2 * len(group)
    expert_rows([0] + first, due=2, send_gate=arrived(2))
    products(paired(rest), *wanted)
    worked = both([0] + first)
    gradients = [None] * 3

    def add_gradients(offsets, chunks_from, kinds, ends):
        deltas = [[done[kind] for done in results[chunks_from:]] for kind in kinds]
        before = [gradients[kind] for kind in kinds if gradients[kind] is not None]
        down = int(kinds[0] == 0)
        made = step(weight_gradients, blocks, offsets, deltas, down, before, ends, bool(down))
        for kind, value in zip(kinds, made):
            gradients[kind] = value

    for i, group in enumerate(groups):
        left = len(groups) - 1 - i
        if left == 1:
            for kind in range(3):
                add_gradients(worked, 0, (kind,), False)
            summed_rows, summed_chunks = len(worked), len(results)
        if left == 0:
            expert_rows(group, core_due=1, gate=sent)
        else:
            gate = arrived(leads[i + 1]) + (sent if left == 1 else [])
            expert_rows(group, core_due=1 if left == 1 else None, gate=gate)
            sent = returned[-len(group) :]
        worked = worked + both(group)
    add_gradients(worked[summed_rows:], summed_chunks, (1, 2), True)
    add_gradients(worked[summed_rows:], summed_chunks, (0,), True)
    down_gradient, gate_gradient, up_gradient = gradients
    layer_output, token_gradient, route_gradient = final_sums(
        payload, returned, width, expert_ids.shape[1], experts, lanes
    )
    return (
        layer_output,
        token_gradient,
        route_gradient.T,
        gate_gradient[None],
        up_gradient[None],
        down_gradient[None],
    )


def solution(mesh):
    by_token = P("expert", "dp")
    by_row = P("expert", None)
    by_weight = P("expert", None, "dp")
    return jax.shard_map(
        local,
        mesh=mesh,
        in_specs=(by_token, by_row, by_row, by_weight, by_weight, by_weight, by_token),
        out_specs=(by_token, by_token, by_row, by_weight, by_weight, by_weight),
        check_vma=False,
    )
```
